32 devices in a mesh: seq: 2 (over core), fsdp: 16 (over z, y, x).
Axes of the slice: x: 2, y: 2, z: 4, core: 2. Of those that a mesh axis runs over, the one named last changes fastest.
Arguments:
- tokens: bfloat16 [64, 492, 768], P('fsdp', 'seq'), may hold values from -8 to 8
- read_memory: bfloat16 [64, 10, 768], P('fsdp'), may hold values from -6 to 6
- valid_count: int32 [64], P('fsdp'), may hold values from 123 to 492, as said below
- cotangent: bfloat16 [64, 512, 768], P('fsdp', 'seq'), may hold values from -6 to 6
- query_weight: bfloat16 [768, 768], P(('seq', 'fsdp')), may hold values from -0.3125 to 0.3125
- query_bias: bfloat16 [768], P(('seq', 'fsdp')), may hold values from -1.75 to 1.75
- key_weight: bfloat16 [768, 768], P(('seq', 'fsdp')), may hold values from -0.3125 to 0.3125
- value_weight: bfloat16 [768, 768], P(('seq', 'fsdp')), may hold values from -0.21875 to 0.21875
- value_bias: bfloat16 [768], P(('seq', 'fsdp')), may hold values from -1.75 to 1.75
- output_weight: bfloat16 [768, 768], P(('seq', 'fsdp')), may hold values from -0.875 to 0.875
- output_bias: bfloat16 [768], P(('seq', 'fsdp')), may hold values from -1.75 to 1.75
- first_gain: bfloat16 [768], P(('seq', 'fsdp')), may hold values from 0.5 to 1.5
- first_shift: bfloat16 [768], P(('seq', 'fsdp')), may hold values from -1.75 to 1.75
- inner_weight: bfloat16 [768, 3072], P(('seq', 'fsdp')), may hold values from -0.21875 to 0.21875
- inner_bias: bfloat16 [3072], P(('seq', 'fsdp')), may hold values from -1.75 to 1.75
- outer_weight: bfloat16 [3072, 768], P(('seq', 'fsdp')), may hold values from -0.109375 to 0.109375
- outer_bias: bfloat16 [768], P(('seq', 'fsdp')), may hold values from -1.75 to 1.75
- second_gain: bfloat16 [768], P(('seq', 'fsdp')), may hold values from 0.5 to 1.5
- second_shift: bfloat16 [768], P(('seq', 'fsdp')), may hold values from -1.75 to 1.75
Outputs:
- layer_out: bfloat16 [64, 512, 768], P('fsdp', 'seq')
- tokens_grad: bfloat16 [64, 492, 768], P('fsdp', 'seq')
- memory_grad: float32 [64, 10, 768], P('fsdp')
- query_weight_grad: float32 [768, 768], P(('seq', 'fsdp'))
- query_bias_grad: float32 [768], P(('seq', 'fsdp'))
- key_weight_grad: float32 [768, 768], P(('seq', 'fsdp'))
- value_weight_grad: float32 [768, 768], P(('seq', 'fsdp'))
- value_bias_grad: float32 [768], P(('seq', 'fsdp'))
- output_weight_grad: float32 [768, 768], P(('seq', 'fsdp'))
- output_bias_grad: float32 [768], P(('seq', 'fsdp'))
- first_gain_grad: float32 [768], P(('seq', 'fsdp'))
- first_shift_grad: float32 [768], P(('seq', 'fsdp'))
- inner_weight_grad: float32 [768, 3072], P(('seq', 'fsdp'))
- inner_bias_grad: float32 [3072], P(('seq', 'fsdp'))
- outer_weight_grad: float32 [3072, 768], P(('seq', 'fsdp'))
- outer_bias_grad: float32 [768], P(('seq', 'fsdp'))
- second_gain_grad: float32 [768], P(('seq', 'fsdp'))
- second_shift_grad: float32 [768], P(('seq', 'fsdp'))
The draws below stay inside these ranges and needn't reach their ends.
Inputs may be any that keep to these rules, and one draw needn't show every extreme that they name: `valid_count`: real tokens of a segment; the first of every 4 segments is full.
All inputs are finite; a program needn't handle non-finite values.
Results may differ from the reference program's by a relative error of at most 0.015.
The reference program's roundings to bfloat16 on the way count: a program that leaves them out, or rounds other values in their place, can miss the bound.
Values may be sent and summed in bfloat16 or wider, within the bound.
No kernel may reach another device: no remote copies, remote signals or barrier semaphores. Data moves between devices by JAX's collectives and lax.ppermute only.
A program may use at most 192 MiB of HBM per device.

```python
import jax
import jax.numpy as jnp
from jax import lax

D = 768
H = 12
HD = 64
FF = 3072
MEM = 10
TOK_SEG = 492
SEG = 512
SEG_DEV = 4
SEGS = 64
N_FSDP = 16


def draw_valid_count(key, part):
    counts = jax.random.randint(key, (SEGS,), TOK_SEG // 4, TOK_SEG + 1)
    leading = jnp.arange(SEGS) % SEG_DEV == 0
    return jnp.where(leading, TOK_SEG, counts).astype(jnp.int32)


def with_spikes(values, key, source, target, parts, factor):
    owner, partner = [(jnp.arange(values.shape[position]) // (values.shape[position] // parts)).reshape([-1 if axis == position else 1 for axis in range(values.ndim)]) for position in (source, target)]
    chosen = jax.random.permutation(key, parts)[partner]
    strong = (owner == chosen) | (owner == (partner + parts // 2) % parts)
    return jnp.where(strong, factor * values, values)


def steps_of(rng, shape, split, low, top_value):
    factor_of = 1.0
    for position, blocks in split:
        steps = jax.random.uniform(jax.random.fold_in(jax.random.fold_in(rng, 6), position), (blocks,), jnp.float32, low / len(split), top_value / len(split))
        factor_of = factor_of * jnp.repeat(jnp.exp(steps), shape[position] // blocks).reshape((-1,) + (1,) * (len(shape) - 1 - position))
    return factor_of


def gaussian(rng, extent, deviation, limit, shards=(), kind=jnp.bfloat16):
    factor_of = steps_of(rng, extent, shards, -0.22, 0.18) if shards else 1.0
    values = jax.random.normal(rng, extent, jnp.float32) * deviation * factor_of
    return jnp.minimum(jnp.maximum(values, -limit), limit).astype(kind)


def heavy_noise(own_key, dims, width, reach, pieces, heavy, dtype=jnp.bfloat16):
    values = width * jax.random.normal(own_key, dims, jnp.float32)
    if pieces:
        values = values * steps_of(own_key, dims, pieces, -0.22, 0.18)
    return jnp.clip(with_spikes(values, jax.random.fold_in(own_key, 3), *heavy), -reach, reach).astype(dtype)


def setup_inputs(seed: int = 0) -> dict:
    streams_of = jax.random.split(jax.random.key(seed), 20)
    tokens = heavy_noise(streams_of[0], (SEGS, TOK_SEG, D), 1.0, 8.0, ((0, 16), (1, 2)), (0, 2, 16, 2.0))
    read_memory = gaussian(streams_of[1], (SEGS, MEM, D), 1.0, 6.0, ((0, 16),))
    valid_count = draw_valid_count(jax.random.fold_in(streams_of[19], 71), 0)
    cotangent = gaussian(streams_of[3], (SEGS, SEG, D), 1.0, 6.0, ((0, 16), (1, 2)))
    query_weight = gaussian(streams_of[4], (D, D), (D // 2) ** -0.5, 0.3125, ((0, 32),))
    query_bias = gaussian(streams_of[5], (D,), 0.3, 1.75, ((0, 32),))
    key_weight = gaussian(streams_of[6], (D, D), (D // 2) ** -0.5, 0.3125, ((0, 32),))
    value_weight = gaussian(streams_of[7], (D, D), D ** -0.5, 0.21875, ((0, 32),))
    value_bias = gaussian(streams_of[8], (D,), 0.3, 1.75, ((0, 32),))
    output_weight = gaussian(streams_of[9], (D, D), (D // 16) ** -0.5, 0.875, ((0, 32),))
    output_bias = gaussian(streams_of[10], (D,), 0.3, 1.75, ((0, 32),))
    first_gain = jnp.clip(1.0 + 0.1 * jax.random.normal(streams_of[11], (D,), jnp.float32), 0.5, 1.5).astype(jnp.bfloat16)
    first_shift = gaussian(streams_of[12], (D,), 0.3, 1.75, ((0, 32),))
    inner_weight = gaussian(streams_of[13], (D, FF), D ** -0.5, 0.21875, ((0, 32),))
    inner_bias = gaussian(streams_of[14], (FF,), 0.3, 1.75, ((0, 32),))
    outer_weight = gaussian(streams_of[15], (FF, D), FF ** -0.5, 0.109375, ((0, 32),))
    outer_bias = gaussian(streams_of[16], (D,), 0.3, 1.75, ((0, 32),))
    second_gain = jnp.clip(1.0 + 0.1 * jax.random.normal(streams_of[17], (D,), jnp.float32), 0.5, 1.5).astype(jnp.bfloat16)
    second_shift = gaussian(streams_of[18], (D,), 0.3, 1.75, ((0, 32),))
    return dict(tokens=tokens, read_memory=read_memory, valid_count=valid_count, cotangent=cotangent, query_weight=query_weight, query_bias=query_bias, key_weight=key_weight, value_weight=value_weight, value_bias=value_bias, output_weight=output_weight, output_bias=output_bias, first_gain=first_gain, first_shift=first_shift, inner_weight=inner_weight, inner_bias=inner_bias, outer_weight=outer_weight, outer_bias=outer_bias, second_gain=second_gain, second_shift=second_shift)


HIGH = lax.Precision.HIGHEST
EPSILON = 1e-12

@jax.custom_vjp
def low(v):
    return lax.optimization_barrier(v.astype(jnp.bfloat16)).astype(jnp.float32)

@jax.custom_vjp
def low_back(v):
    return v

def low_keep(v):
    return (low(v), None)

def low_pass(kept, grad):
    return (grad,)

def back_keep(v):
    return (v, None)

def back_low(kept, grad):
    return (low(grad),)
low.defvjp(low_keep, low_pass)
low_back.defvjp(back_keep, back_low)

def norm_layer(resid, gain, shift):
    centre = resid - lax.optimization_barrier(jnp.mean(resid, axis=-1, keepdims=True))
    spread = lax.optimization_barrier(jnp.mean(centre * centre, axis=-1, keepdims=True))
    return centre * lax.rsqrt(spread + EPSILON) * gain + shift

def project(inputs, weight):
    return jnp.einsum('srd,de->sre', inputs, weight, precision=HIGH)

def key_keep(valid):
    places = jnp.arange(SEG)[None, :]
    return (places < MEM) | (places >= SEG - MEM) | (places - MEM < valid[:, None])

def layer(weights, tok_rows, mem_rows, valid):
    query_weight, query_bias, key_weight, value_weight, value_bias, output_weight, output_bias, first_gain, first_shift, inner_weight, inner_bias, outer_weight, outer_bias, second_gain, second_shift = weights
    rows = jnp.concatenate([mem_rows, tok_rows, mem_rows], axis=1)
    count = rows.shape[0]
    query = low_back(low(project(rows, query_weight) + query_bias))
    keys = low_back(low(project(rows, key_weight)))
    values = low_back(low(project(rows, value_weight) + value_bias))
    query_h = query.reshape(count, SEG, H, HD)
    keys_h = keys.reshape(count, SEG, H, HD)
    values_h = values.reshape(count, SEG, H, HD)
    scores = low_back(jnp.einsum('sqhe,skhe->shqk', query_h, keys_h, precision=HIGH) * HD ** (-0.5))
    keep = key_keep(valid)
    masked = jnp.where(keep[:, None, None, :], scores, -1000000000.0)
    probs = jax.nn.softmax(masked, axis=-1)
    mixed = jnp.einsum('shqk,skhe->sqhe', low(probs), values_h, precision=HIGH)
    attended = low_back(low(mixed.reshape(count, SEG, D)))
    branch = low_back(project(attended, output_weight) + output_bias)
    first = norm_layer(rows + branch, first_gain, first_shift)
    inner = low_back(project(low(first), inner_weight) + inner_bias)
    active = low(jax.nn.gelu(inner, approximate=False))
    outer = low_back(project(active, outer_weight) + outer_bias)
    return norm_layer(first + outer, second_gain, second_shift)

def group(array):
    return array.reshape((N_FSDP, SEG_DEV) + array.shape[1:])

def reference(tokens, read_memory, valid_count, cotangent, query_weight, query_bias, key_weight, value_weight, value_bias, output_weight, output_bias, first_gain, first_shift, inner_weight, inner_bias, outer_weight, outer_bias, second_gain, second_shift):
    params = (query_weight, query_bias, key_weight, value_weight, value_bias, output_weight, output_bias, first_gain, first_shift, inner_weight, inner_bias, outer_weight, outer_bias, second_gain, second_shift)
    params = tuple((weight.astype(jnp.float32) for weight in params))

    def advance(totals, items):
        tok_part, mem_part, valid_part, cot_part = items

        def forward(weights, tok_rows, mem_rows):
            return layer(weights, tok_rows, mem_rows, valid_part)
        result, pullback = jax.vjp(forward, params, tok_part.astype(jnp.float32), mem_part.astype(jnp.float32))
        grads, tok_grad, mem_grad = pullback(cot_part.astype(jnp.float32))
        totals = tuple((total + grad for total, grad in zip(totals, grads)))
        return (totals, (result.astype(jnp.bfloat16), tok_grad.astype(jnp.bfloat16), mem_grad))
    zero_grads = tuple((jnp.zeros_like(weight) for weight in params))
    totals, (results, tok_grads, mem_grads) = lax.scan(advance, zero_grads, (group(tokens), group(read_memory), group(valid_count), group(cotangent)))
    layer_out = results.reshape((SEGS,) + results.shape[2:])
    tokens_grad = tok_grads.reshape((SEGS,) + tok_grads.shape[2:])
    memory_grad = mem_grads.reshape((SEGS,) + mem_grads.shape[2:])
    return (layer_out, tokens_grad, memory_grad, totals[0], totals[1], totals[2], totals[3], totals[4], totals[5], totals[6], totals[7], totals[8], totals[9], totals[10], totals[11], totals[12], totals[13], totals[14])
```

```python
import math

import jax
import jax.numpy as jnp
from jax import lax
from jax.experimental import pallas as pl
from jax.experimental.pallas import tpu as pltpu
from jax.sharding import PartitionSpec as P

HD = 64
MEM = 10
SEG = 512
BF = jnp.bfloat16
F32 = jnp.float32

EPSILON = 1e-12
ROOT_HALF = math.sqrt(0.5)
INV_ROOT_TAU = 1.0 / math.sqrt(2.0 * math.pi)
AXES = ("seq", "fsdp")


def normalize(resid):
    centre = resid - jnp.mean(resid, axis=-1, keepdims=True)
    inverse = lax.rsqrt(jnp.mean(centre * centre, axis=-1, keepdims=True) + EPSILON)
    return (centre * inverse, inverse)


def norm_back(grad_out, normed, inverse, gain):
    scaled = grad_out * gain
    return inverse * (
        scaled
        - jnp.mean(scaled, axis=-1, keepdims=True)
        - normed * jnp.mean(scaled * normed, axis=-1, keepdims=True)
    )


def gelu_slope(inner):
    return (
        0.5 * (1.0 + lax.erf(inner * ROOT_HALF))
        + inner * jnp.exp(-0.5 * inner * inner) * INV_ROOT_TAU
    )


def dot(a, b):
    return jnp.dot(a, b, preferred_element_type=F32)


def dot_nt(a, b):
    return lax.dot_general(a, b, (((1,), (1,)), ((), ())), preferred_element_type=F32)


def dot_tn(a, b):
    return lax.dot_general(a, b, (((0,), (0,)), ((), ())), preferred_element_type=F32)


def hop(x, bit):
    size = lax.axis_size("fsdp")
    return lax.ppermute(x, "fsdp", [(i, i ^ bit) for i in range(size)])


def hop_core(x):
    return lax.ppermute(x, "seq", [(0, 1), (1, 0)])


ORDER_A = [b + x + y for y in (0, 2) for x in (0, 1) for b in (0, 4, 8, 12)]
ORDER_B = [b + x + y for x in (0, 1) for y in (0, 2) for b in (0, 4, 8, 12)]


def place_kernel(a_ref, b_ref, ac_ref, bc_ref, out_ref, sem):
    side = lax.axis_index("seq")
    me = lax.axis_index("fsdp")
    half = a_ref.shape[1]
    copies = []
    for order, low, mine, other in (
        (ORDER_A, 0, a_ref, ac_ref),
        (ORDER_B, half, b_ref, bc_ref),
    ):
        for j, bits in enumerate(order):
            at = jnp.bitwise_xor(me, bits)
            for src, core in ((mine, side), (other, 1 - side)):
                copies.append(
                    pltpu.make_async_copy(
                        src.at[j],
                        out_ref.at[core * 16 + at, low : low + half],
                        sem.at[len(copies)],
                    )
                )
    for copy in copies:
        copy.start()
    for copy in copies:
        copy.wait()


def gather_group(x):
    half = x.shape[0] // 2
    z = jnp.stack([x] + [hop(x, b) for b in (4, 8, 12)])
    a, b = z[:, :half], z[:, half:]
    ax, by = hop(a, 1), hop(b, 2)
    a2, b2 = jnp.concatenate([a, ax]), jnp.concatenate([b, by])
    ay, bx = hop(a2, 2), hop(b2, 1)
    a3, b3 = jnp.concatenate([a2, ay]), jnp.concatenate([b2, bx])
    ac, bc = hop_core(a3), hop_core(b3)
    shape = (32,) + x.shape
    return pl.pallas_call(
        place_kernel,
        out_shape=jax.ShapeDtypeStruct(shape, x.dtype),
        in_specs=[pl.BlockSpec(memory_space=pl.ANY)] * 4,
        out_specs=pl.BlockSpec(memory_space=pl.ANY),
        scratch_shapes=[pltpu.SemaphoreType.DMA((64,))],
        cost_estimate=pl.CostEstimate(
            flops=0, transcendentals=0, bytes_accessed=128 * x.size
        ),
    )(a3, b3, ac, bc)


def part(x, index, axis):
    return lax.dynamic_index_in_dim(x, index, axis, keepdims=False)


def add_low(*terms):
    total = terms[0].astype(F32)
    for term in terms[1:]:
        total = total + term.astype(F32)
    return total.astype(BF)


def scatter_group(g):
    side = lax.axis_index("seq")
    me = lax.axis_index("fsdp")
    zi, yi, xi = me // 4, (me // 2) % 2, me % 2
    units = g.shape[1]
    half = units // 2
    g = g.reshape((2, 4, 2, 2) + g.shape[1:])
    got = hop_core(part(g, 1 - side, 0))
    s = add_low(part(g, side, 0), got)
    a, b = s[:, :, :, :half], s[:, :, :, half:]
    ga, gb = hop(part(a, 1 - yi, 1), 2), hop(part(b, 1 - xi, 2), 1)
    a, b = add_low(part(a, yi, 1), ga), add_low(part(b, xi, 2), gb)
    ga, gb = hop(part(a, 1 - xi, 1), 1), hop(part(b, 1 - yi, 1), 2)
    s = jnp.concatenate(
        [add_low(part(a, xi, 1), ga), add_low(part(b, yi, 1), gb)], axis=1
    )
    got = [hop(part(s, jnp.bitwise_xor(zi, d), 0), 4 * d) for d in (1, 2, 3)]
    total = part(s, zi, 0).astype(F32)
    for term in got:
        total = total + term.astype(F32)
    return total


def key_keep(valid):
    places = jnp.arange(SEG)
    return (places < MEM) | (places >= SEG - MEM) | (places - MEM < valid)


def head_split(block):
    return block.reshape(block.shape[0], -1, HD)


def segment_scores(query, keys, valid):
    query_h = head_split(query)
    keys_h = head_split(keys)
    scores = jnp.einsum(
        "qhe,khe->hqk", query_h, keys_h, preferred_element_type=F32
    ) * HD ** (-0.5)
    keep = key_keep(valid)
    return jnp.where(keep[None, None, :], scores, -1000000000.0), query_h, keys_h


def attend_segment(query, keys, values, valid):
    scores, _, _ = segment_scores(query, keys, valid)
    top = jnp.max(scores, axis=-1, keepdims=True)
    weights = jnp.exp(scores - top)
    total = jnp.sum(weights, axis=-1, keepdims=True)
    probs = weights / total
    mixed = jnp.einsum(
        "hqk,khe->qhe", probs.astype(BF), head_split(values), preferred_element_type=F32
    )
    return mixed.reshape(SEG, -1).astype(BF), (top + jnp.log(total))[..., 0]


def attend_back(query, keys, values, grad_mixed, log_total, valid):
    scores, query_h, keys_h = segment_scores(query, keys, valid)
    probs = jnp.exp(scores - log_total[..., None])
    grad_h = head_split(grad_mixed)
    grad_probs = jnp.einsum(
        "qhe,khe->hqk", grad_h, head_split(values), preferred_element_type=F32
    )
    delta = jnp.sum(probs * grad_probs, axis=-1, keepdims=True)
    grad_scores = (probs * (grad_probs - delta)).astype(BF)
    scale = HD ** (-0.5)
    grad_query = (
        jnp.einsum("hqk,khe->qhe", grad_scores, keys_h, preferred_element_type=F32)
        * scale
    )
    grad_keys = (
        jnp.einsum("hqk,qhe->khe", grad_scores, query_h, preferred_element_type=F32)
        * scale
    )
    grad_values = jnp.einsum(
        "hqk,qhe->khe", probs.astype(BF), grad_h, preferred_element_type=F32
    )
    return tuple(
        g.reshape(SEG, -1).astype(BF) for g in (grad_query, grad_keys, grad_values)
    )


def column_sum(values):
    return jnp.sum(values.astype(F32), axis=0)


VECTORS = (
    "query_bias",
    "value_bias",
    "output_bias",
    "first_gain",
    "first_shift",
    "outer_bias",
    "second_gain",
    "second_shift",
)


def split_columns(w, width):
    return jnp.stack([w[:, i : i + width] for i in range(0, w.shape[1], width)])


def gather_params(p, ring):
    if not ring:
        full = {
            name: lax.all_gather(value, AXES, axis=0, tiled=True)
            for name, value in p.items()
        }
        return full
    width = p["query_weight"].shape[1]
    rows = p["query_weight"].shape[0]
    vec = jnp.concatenate([p[n] for n in VECTORS] + [p["inner_bias"]])
    room = rows * width
    vec = jnp.pad(vec, (0, width - vec.shape[0])).reshape(1, width)
    vec = jnp.pad(vec, ((0, rows - 1), (0, 0)))
    del room
    first = gather_group(
        jnp.stack([p["query_weight"], p["key_weight"], p["value_weight"], vec])
    )
    second = gather_group(
        jnp.concatenate(
            [p["output_weight"][None], split_columns(p["inner_weight"], width),
             jnp.zeros((1, rows, width), BF)]
        )
    )
    third = gather_group(p["outer_weight"].reshape(4, -1, width))
    full = {}
    for i, name in enumerate(("query_weight", "key_weight", "value_weight")):
        full[name] = first[:, i].reshape(-1, width)
    got = first[:, 3, 0]
    for i, name in enumerate(VECTORS):
        full[name] = got[:, i * rows : (i + 1) * rows].reshape(-1)
    at = len(VECTORS) * rows
    full["inner_bias"] = got[:, at : at + p["inner_bias"].shape[0]].reshape(-1)
    full["output_weight"] = second[:, 0].reshape(-1, width)
    full["inner_weight"] = jnp.concatenate(
        [second[:, 1 + i].reshape(-1, width) for i in range(4)], axis=1
    )
    full["outer_weight"] = third.reshape(-1, width)
    return full


def layer_pass(w, rows, cot, valid):
    count, seg, width = rows.shape
    flat = rows.reshape(-1, width)
    query = (dot(flat, w["query_weight"]) + w["query_bias"].astype(F32)).astype(BF)
    keys = dot(flat, w["key_weight"]).astype(BF)
    values = (dot(flat, w["value_weight"]) + w["value_bias"].astype(F32)).astype(BF)
    mixed, logs = [], []
    for s in range(count):
        cut = slice(s * seg, (s + 1) * seg)
        m, lt = attend_segment(query[cut], keys[cut], values[cut], valid[s])
        mixed.append(m)
        logs.append(lt)
    attended = jnp.concatenate(mixed)
    branch = dot(attended, w["output_weight"]) + w["output_bias"].astype(F32)
    normed_one, inverse_one = normalize(flat.astype(F32) + branch)
    first = normed_one * w["first_gain"].astype(F32) + w["first_shift"].astype(F32)
    first_low = first.astype(BF)
    inner = dot(first_low, w["inner_weight"]) + w["inner_bias"].astype(F32)
    active = jax.nn.gelu(inner, approximate=False).astype(BF)
    outer = dot(active, w["outer_weight"]) + w["outer_bias"].astype(F32)
    normed_two, inverse_two = normalize(first + outer)
    result = (
        normed_two * w["second_gain"].astype(F32) + w["second_shift"].astype(F32)
    ).astype(BF)
    grad_out = cot.reshape(-1, width).astype(F32)
    g = {}
    g["second_gain"] = jnp.sum(grad_out * normed_two, axis=0)
    g["second_shift"] = jnp.sum(grad_out, axis=0)
    grad_res_two = norm_back(
        grad_out, normed_two, inverse_two, w["second_gain"].astype(F32)
    )
    grad_outer = grad_res_two.astype(BF)
    g["outer_bias"] = column_sum(grad_outer)
    g["outer_weight"] = dot_tn(active, grad_outer)
    grad_active = dot_nt(grad_outer, w["outer_weight"])
    grad_inner = (grad_active * gelu_slope(inner)).astype(BF)
    g["inner_bias"] = column_sum(grad_inner)
    g["inner_weight"] = dot_tn(first_low, grad_inner)
    grad_first = grad_res_two + dot_nt(grad_inner, w["inner_weight"])
    g["first_gain"] = jnp.sum(grad_first * normed_one, axis=0)
    g["first_shift"] = jnp.sum(grad_first, axis=0)
    grad_res_one = norm_back(
        grad_first, normed_one, inverse_one, w["first_gain"].astype(F32)
    )
    grad_branch = grad_res_one.astype(BF)
    g["output_bias"] = column_sum(grad_branch)
    g["output_weight"] = dot_tn(attended, grad_branch)
    grad_attended = dot_nt(grad_branch, w["output_weight"]).astype(BF)
    parts = []
    for s in range(count):
        cut = slice(s * seg, (s + 1) * seg)
        parts.append(
            attend_back(
                query[cut], keys[cut], values[cut], grad_attended[cut], logs[s], valid[s]
            )
        )
    grad_query, grad_keys, grad_values = (
        jnp.concatenate([q[i] for q in parts]) for i in range(3)
    )
    g["query_weight"] = dot_tn(flat, grad_query)
    g["query_bias"] = column_sum(grad_query)
    g["key_weight"] = dot_tn(flat, grad_keys)
    g["value_weight"] = dot_tn(flat, grad_values)
    g["value_bias"] = column_sum(grad_values)
    grad_rows = (
        grad_res_one
        + dot_nt(grad_query, w["query_weight"])
        + dot_nt(grad_keys, w["key_weight"])
        + dot_nt(grad_values, w["value_weight"])
    )
    return (
        result.reshape(rows.shape),
        grad_rows.reshape(rows.shape),
        g,
    )


NAMES = (
    "query_weight",
    "query_bias",
    "key_weight",
    "value_weight",
    "value_bias",
    "output_weight",
    "output_bias",
    "first_gain",
    "first_shift",
    "inner_weight",
    "inner_bias",
    "outer_weight",
    "outer_bias",
    "second_gain",
    "second_shift",
)


def scatter_params(g, ring):
    if not ring:
        return {
            name: lax.psum_scatter(value, AXES, scatter_dimension=0, tiled=True)
            for name, value in g.items()
        }
    width = g["query_weight"].shape[1]
    low = {n: v.astype(BF) for n, v in g.items()}
    rows = width // 32
    out = {}
    out["outer_weight"] = scatter_group(
        low["outer_weight"].reshape(32, 4, -1, width)
    ).reshape(-1, width)
    inner = jnp.stack(
        [
            low["inner_weight"][:, i * width : (i + 1) * width].reshape(32, rows, width)
            for i in range(4)
        ],
        axis=1,
    )
    got = scatter_group(inner)
    out["inner_weight"] = jnp.concatenate([got[i] for i in range(4)], axis=1)
    vec = jnp.concatenate(
        [low[n].reshape(32, -1) for n in VECTORS] + [low["inner_bias"].reshape(32, -1)],
        axis=1,
    )
    used = vec.shape[1]
    vec = jnp.pad(vec, ((0, 0), (0, width - used))).reshape(32, 1, 1, width)
    vec = jnp.pad(vec, ((0, 0), (0, 0), (0, rows - 1), (0, 0)))
    names = ("output_weight", "value_weight", "key_weight", "query_weight")
    stack = jnp.stack([low[n].reshape(32, rows, width) for n in names], axis=1)
    got = scatter_group(jnp.concatenate([stack, vec, jnp.zeros_like(vec)], axis=1))
    for i, n in enumerate(names):
        out[n] = got[i]
    got = got[4, 0]
    for i, n in enumerate(VECTORS):
        out[n] = got[i * rows : (i + 1) * rows]
    at = len(VECTORS) * rows
    out["inner_bias"] = got[at:used]
    return out


def per_device(tokens, read_memory, valid_count, cotangent, *params):
    side = lax.axis_index("seq")
    ring = lax.axis_size("fsdp") == 16
    p = dict(zip(NAMES, params))
    half = tokens.shape[0] // 2
    near = side * half
    far = (1 - side) * half

    def take(x, at):
        return lax.dynamic_slice_in_dim(x, at, half, axis=0)

    def merge(x):
        own, got = take(x, near), hop_core(take(x, far))
        return jnp.where(side == 0, own, got), jnp.where(side == 0, got, own)

    mem = take(read_memory, near)
    valid = take(valid_count, near)
    low_tok, high_tok = merge(tokens)
    rows = jnp.concatenate([mem, low_tok, high_tok, mem], axis=1)
    cot = jnp.concatenate(merge(cotangent), axis=1)

    full = gather_params(p, ring)
    result, grad_rows, grads = layer_pass(full, rows, cot, valid)

    def back(low, high):
        own = jnp.where(side == 0, low, high)
        got = hop_core(jnp.where(side == 0, high, low))
        return jnp.concatenate(
            [jnp.where(side == 0, own, got), jnp.where(side == 0, got, own)]
        )

    mid = SEG // 2
    layer_out = back(result[:, :mid], result[:, mid:])
    grad_low = grad_rows.astype(BF)
    tokens_grad = back(grad_low[:, MEM:mid], grad_low[:, mid : SEG - MEM])
    grad_mem = grad_rows[:, :MEM] + grad_rows[:, SEG - MEM :]
    got = hop_core(grad_mem)
    memory_grad = jnp.concatenate(
        [jnp.where(side == 0, grad_mem, got), jnp.where(side == 0, got, grad_mem)]
    )
    shards = scatter_params(grads, ring)
    return (layer_out, tokens_grad, memory_grad) + tuple(shards[n] for n in NAMES)


def solution(mesh):
    row = P("fsdp", "seq", None)
    whole = P("fsdp", None, None)
    mat, vec = P(AXES, None), P(AXES)
    specs = tuple(mat if n.endswith("_weight") else vec for n in NAMES)
    return jax.shard_map(
        per_device,
        mesh=mesh,
        in_specs=(row, whole, P("fsdp"), row) + specs,
        out_specs=(row, row, whole) + specs,
        check_vma=False,
    )
```

```python
import functools
import math

import jax
import jax.numpy as jnp
from jax import lax
from jax.experimental import pallas as pl
from jax.experimental.pallas import tpu as pltpu
from jax.sharding import PartitionSpec as P

HD = 64
MEM = 10
SEG = 512
LANES = 128
BLOCK = 256
BF = jnp.bfloat16
F32 = jnp.float32

EPSILON = 1e-12
ROOT_HALF = math.sqrt(0.5)
INV_ROOT_TAU = 1.0 / math.sqrt(2.0 * math.pi)
AXES = ("seq", "fsdp")
NAMES = "Wq bq Wk Wv bv Wo bo g1 s1 W1 b1 W2 b2 g2 s2".split()
VECTORS = "bq bv bo g1 s1 b2 g2 s2".split()
VMEM_LIMIT = 60 * 1024 * 1024

ANY = pl.BlockSpec(memory_space=pl.ANY)


def dot(a, b):
    return jnp.dot(a, b, preferred_element_type=F32)


def dot_nt(a, b):
    return lax.dot_general(a, b, (((1,), (1,)), ((), ())), preferred_element_type=F32)


def dot_tn(a, b):
    return lax.dot_general(a, b, (((0,), (0,)), ((), ())), preferred_element_type=F32)


def cost(flops, moved, transcendentals=0):
    return pl.CostEstimate(
        flops=int(flops),
        bytes_accessed=int(moved),
        transcendentals=int(transcendentals),
    )


def params(**more):
    return pltpu.CompilerParams(vmem_limit_bytes=VMEM_LIMIT, **more)


def once(shape, index):
    return pl.BlockSpec(shape, index, pipeline_mode=pl.Buffered(1))


def hop(x, bit):
    size = lax.axis_size("fsdp")
    return lax.ppermute(x, "fsdp", [(i, i ^ bit) for i in range(size)])


def hop_core(x):
    return lax.ppermute(x, "seq", [(0, 1), (1, 0)])


def place():
    me = lax.axis_index("fsdp")
    return me // 4, (me // 2) % 2, me % 2


def pair(bit, mine, got, axis):
    return jnp.stack(
        [jnp.where(bit == 0, mine, got), jnp.where(bit == 0, got, mine)], axis=axis
    )


def gather_group(x):
    zi, yi, xi = place()
    rows, columns = x.shape
    half = columns // 2 // LANES * LANES
    z = [x] + [hop(x, 4 * d) for d in (1, 2, 3)]
    z = jnp.stack(
        [
            jnp.where(
                zi < 2,
                jnp.where(zi == 0, z[i], z[i ^ 1]),
                jnp.where(zi == 2, z[i ^ 2], z[i ^ 3]),
            )
            for i in range(4)
        ]
    )
    a, b = z[:, :, :half], z[:, :, half:]
    a, b = pair(xi, a, hop(a, 1), 1), pair(yi, b, hop(b, 2), 1)
    a, b = pair(yi, a, hop(a, 2), 1), pair(xi, b, hop(b, 1), 2)
    a, b = a.reshape(16 * rows, -1), b.reshape(16 * rows, -1)
    return a, hop_core(a), b, hop_core(b)


def part(x, index, axis):
    return lax.dynamic_index_in_dim(x, index, axis, keepdims=False)


def add_low(*terms):
    total = terms[0].astype(F32)
    for term in terms[1:]:
        total = total + term.astype(F32)
    return total.astype(BF)


def scatter_group(send, keep):
    zi, yi, xi = place()
    columns = send.shape[1]
    half = columns // 2 // LANES * LANES
    s = add_low(keep, hop_core(send)).reshape(4, 2, 2, -1, columns)
    a, b = s[..., :half], s[..., half:]
    ga, gb = hop(part(a, 1 - yi, 1), 2), hop(part(b, 1 - xi, 2), 1)
    a, b = add_low(part(a, yi, 1), ga), add_low(part(b, xi, 2), gb)
    ga, gb = hop(part(a, 1 - xi, 1), 1), hop(part(b, 1 - yi, 1), 2)
    s = jnp.concatenate(
        [add_low(part(a, xi, 1), ga), add_low(part(b, yi, 1), gb)], axis=-1
    )
    got = [hop(part(s, jnp.bitwise_xor(zi, d), 0), 4 * d) for d in (1, 2, 3)]
    total = part(s, zi, 0).astype(F32)
    for term in got:
        total = total + term.astype(F32)
    return total


def fetch(pieces, target, sem, at):
    side = lax.axis_index("seq")
    rows = target.shape[0] // 2
    half = pieces[0].shape[1]
    copies = []
    for i, piece in enumerate(pieces):
        core = side if i % 2 == 0 else 1 - side
        start = pl.multiple_of(core * rows, 16)
        columns = slice(0, half) if i < 2 else slice(half, target.shape[1])
        copies.append(
            pltpu.make_async_copy(
                piece, target.at[pl.ds(start, rows), columns], sem.at[at + i]
            )
        )
    return copies


def project_kernel(x_ref, bias_ref, *refs):
    pieces, (q_ref, k_ref, v_ref), (w, sem) = refs[:4], refs[-5:-2], refs[-2:]
    width = x_ref.shape[1]

    @pl.when(pl.program_id(0) == 0)
    def _():
        copies = fetch(pieces, w, sem, 0)
        for copy in copies:
            copy.start()
        for copy in copies:
            copy.wait()

    x = x_ref[...]
    q = (dot(x, w[:, :width]) + bias_ref[0:1, :]).astype(BF)
    q_ref[...] = (q.astype(F32) * HD ** (-0.5)).astype(BF)
    k_ref[...] = dot(x, w[:, width : 2 * width]).astype(BF)
    v_ref[...] = (dot(x, w[:, 2 * width : 3 * width]) + bias_ref[1:2, :]).astype(BF)


def project(flat, bias, pieces, after):
    rows, width = flat.shape
    columns = pieces[0].shape[1] + pieces[2].shape[1]
    block = pl.BlockSpec((BLOCK, width), lambda i: (i, 0))
    out = jax.ShapeDtypeStruct(flat.shape, BF)
    return pl.pallas_call(
        project_kernel,
        grid=(rows // BLOCK,),
        out_shape=(out,) * 3,
        in_specs=[block, once(bias.shape, lambda i: (0, 0))] + [ANY] * (4 + len(after)),
        out_specs=(block,) * 3,
        scratch_shapes=[
            pltpu.VMEM((width, columns), BF),
            pltpu.SemaphoreType.DMA((4,)),
        ],
        compiler_params=params(),
        cost_estimate=cost(6 * rows * width * width, 20 * rows * width),
        name="project",
    )(flat, bias, *pieces, *after)


def lane_masks(rows):
    lane = lax.broadcasted_iota(jnp.int32, (rows, LANES), 1)
    return [lane < HD, lane >= HD]


def key_bias(valid):
    at = lax.broadcasted_iota(jnp.int32, (SEG, 1), 0)
    keep = (at < MEM) | (at >= SEG - MEM) | (at - MEM < valid)
    return jnp.where(keep, 0.0, -1000000000.0)


def attend_kernel(valid_ref, q_ref, k_ref, v_ref, *refs):
    o_ref, log_ref = refs[-2:]
    bias = key_bias(valid_ref[pl.program_id(0)])
    q, k, v = q_ref[...], k_ref[...], v_ref[...]
    zero = jnp.zeros_like(q)
    vt = v.T
    outs = []
    for h, mask in enumerate(lane_masks(SEG)):
        scores = dot_nt(k, jnp.where(mask, q, zero)) + bias
        top = jnp.max(scores, axis=0, keepdims=True)
        weights = jnp.exp(scores - top)
        total = jnp.sum(weights, axis=0, keepdims=True)
        probs = (weights * (1.0 / total)).astype(BF)
        outs.append(dot(vt[h * HD : (h + 1) * HD], probs))
        log_ref[0, h : h + 1, :] = top + jnp.log(total)
    o_ref[...] = jnp.concatenate(outs, axis=0).T.astype(BF)


def attend(valid, q, k, v, after):
    rows, width = q.shape
    count, pairs = rows // SEG, width // LANES
    block = pl.BlockSpec((SEG, LANES), lambda s, p, _: (s, p))
    return pl.pallas_call(
        attend_kernel,
        grid_spec=pltpu.PrefetchScalarGridSpec(
            num_scalar_prefetch=1,
            grid=(count, pairs),
            in_specs=[block] * 3 + [ANY] * len(after),
            out_specs=[
                block,
                pl.BlockSpec((1, 8, SEG), lambda s, p, _: (s * pairs + p, 0, 0)),
            ],
        ),
        out_shape=(
            jax.ShapeDtypeStruct(q.shape, BF),
            jax.ShapeDtypeStruct((count * pairs, 8, SEG), F32),
        ),
        compiler_params=params(),
        cost_estimate=cost(16 * rows * SEG * width, 8 * rows * width),
        name="attend",
    )(valid, q, k, v, *after)


def attend_back_kernel(valid_ref, q_ref, k_ref, v_ref, g_ref, log_ref, *refs):
    out_ref, sum_ref = refs[-2:]
    bias = key_bias(valid_ref[pl.program_id(0)])
    q, k, v, g = q_ref[...], k_ref[...], v_ref[...], g_ref[...]
    zero = jnp.zeros_like(q)
    kt = k.T
    gq, gk, gv = [], [], []
    masks = lane_masks(SEG)
    for h, mask in enumerate(masks):
        scores = dot_nt(k, jnp.where(mask, q, zero)) + bias
        probs = jnp.exp(scores - log_ref[0, h : h + 1, :])
        g_probs = dot_nt(v, jnp.where(mask, g, zero))
        delta = jnp.sum(probs * g_probs, axis=0, keepdims=True)
        g_scores = (probs * (g_probs - delta)).astype(BF)
        gv.append(dot(probs.astype(BF), g))
        gk.append(dot(g_scores, q))
        gq.append(dot(kt[h * HD : (h + 1) * HD], g_scores))
    gq = (jnp.concatenate(gq, axis=0).T * HD ** (-0.5)).astype(BF)
    gk = jnp.where(masks[0], gk[0], gk[1]).astype(BF)
    gv = jnp.where(masks[0], gv[0], gv[1]).astype(BF)
    out_ref[0], out_ref[1], out_ref[2] = gq, gk, gv
    sum_ref[...] = jnp.concatenate(
        [
            jnp.sum(gq.astype(F32), axis=0, keepdims=True),
            jnp.sum(gv.astype(F32), axis=0, keepdims=True),
            jnp.zeros((6, LANES), F32),
        ],
        axis=0,
    )[None]


def attend_back(valid, q, k, v, g, logs, after):
    rows, width = q.shape
    count, pairs = rows // SEG, width // LANES
    block = pl.BlockSpec((SEG, LANES), lambda s, p, _: (s, p))
    return pl.pallas_call(
        attend_back_kernel,
        grid_spec=pltpu.PrefetchScalarGridSpec(
            num_scalar_prefetch=1,
            grid=(count, pairs),
            in_specs=[block] * 4
            + [pl.BlockSpec((1, 8, SEG), lambda s, p, _: (s * pairs + p, 0, 0))]
            + [ANY] * len(after),
            out_specs=[
                pl.BlockSpec((3, SEG, LANES), lambda s, p, _: (0, s, p)),
                pl.BlockSpec((1, 8, LANES), lambda s, p, _: (s, 0, p)),
            ],
        ),
        out_shape=(
            jax.ShapeDtypeStruct((3,) + q.shape, BF),
            jax.ShapeDtypeStruct((count, 8, width), F32),
        ),
        compiler_params=params(),
        cost_estimate=cost(40 * rows * SEG * width, 14 * rows * width),
        name="attend_back",
    )(valid, q, k, v, g, logs, *after)


def normalize(resid):
    centre = resid - jnp.mean(resid, axis=-1, keepdims=True)
    inverse = lax.rsqrt(jnp.mean(centre * centre, axis=-1, keepdims=True) + EPSILON)
    return centre * inverse, inverse


def norm_back(grad_out, normed, inverse, gain):
    scaled = grad_out * gain
    return inverse * (
        scaled
        - jnp.mean(scaled, axis=-1, keepdims=True)
        - normed * jnp.mean(scaled * normed, axis=-1, keepdims=True)
    )


def gelu_parts(inner):
    phi = 0.5 * (1.0 + lax.erf(inner * ROOT_HALF))
    slope = phi + inner * (jnp.exp(-0.5 * inner * inner) * INV_ROOT_TAU)
    return inner * phi, slope


def row_sum(x):
    return jnp.sum(x, axis=0, keepdims=True)


def accumulate(ref, rows):
    stack = jnp.concatenate(
        rows + [jnp.zeros((8 - len(rows), rows[0].shape[1]), F32)], axis=0
    )

    @pl.when(pl.program_id(0) == 0)
    def _():
        ref[...] = stack

    @pl.when(pl.program_id(0) != 0)
    def _():
        ref[...] += stack


def forward_kernel(att_ref, x_ref, cot_ref, vec_ref, *refs):
    mid, low = refs[:4], refs[4:8]
    (
        out_ref, first_ref, n1_ref, inv_ref, act_ref, slope_ref, res_ref, gout_ref, sum_ref,
        w1, w2, sem,
    ) = refs[-12:]
    width = x_ref.shape[1]
    step = pl.program_id(0)
    copies = fetch(mid, w1, sem, 0) + fetch(low, w2, sem, 4)

    @pl.when(step == 0)
    def _():
        for copy in copies:
            copy.start()
        for copy in copies:
            copy.wait()

    vec = lambda i: vec_ref[i : i + 1, :]
    branch = dot(att_ref[...], w1[:, :width]) + vec(2)
    n1, inv1 = normalize(x_ref[...].astype(F32) + branch)
    first = n1 * vec(3) + vec(4)
    first_low = first.astype(BF)
    n1_ref[...] = n1
    inv_ref[...] = jnp.broadcast_to(inv1, inv_ref.shape)
    first_ref[...] = first_low
    outer = vec(5)
    for f in range(4):
        cut = slice(f * width, (f + 1) * width)
        inner = dot(first_low, w1[:, (f + 1) * width : (f + 2) * width]) + vec(8 + f)
        active, slope = gelu_parts(inner)
        active = active.astype(BF)
        act_ref[:, cut] = active
        slope_ref[:, cut] = slope
        outer = outer + dot(active, w2[cut, :])
    n2, inv2 = normalize(first + outer)
    out_ref[...] = (n2 * vec(6) + vec(7)).astype(BF)
    cot = cot_ref[...].astype(F32)
    res = norm_back(cot, n2, inv2, vec(6))
    res_ref[...] = res
    gout = res.astype(BF)
    gout_ref[...] = gout
    accumulate(sum_ref, [row_sum(cot * n2), row_sum(cot), row_sum(gout.astype(F32))])


def forward(att, flat, cot, vec, mid, low, after):
    rows, width = flat.shape
    block = pl.BlockSpec((BLOCK, width), lambda i: (i, 0))
    wide = pl.BlockSpec((BLOCK, 4 * width), lambda i: (i, 0))
    narrow = pl.BlockSpec((BLOCK, LANES), lambda i: (i, 0))
    sums = pl.BlockSpec((8, width), lambda i: (0, 0))
    s = jax.ShapeDtypeStruct
    return pl.pallas_call(
        forward_kernel,
        grid=(rows // BLOCK,),
        in_specs=[block] * 3
        + [once(vec.shape, lambda i: (0, 0))]
        + [ANY] * (8 + len(after)),
        out_specs=(block, block, block, narrow, wide, wide, block, block, sums),
        out_shape=(
            s((rows, width), BF),
            s((rows, width), BF),
            s((rows, width), F32),
            s((rows, LANES), F32),
            s((rows, 4 * width), BF),
            s((rows, 4 * width), F32),
            s((rows, width), F32),
            s((rows, width), BF),
            s((8, width), F32),
        ),
        scratch_shapes=[
            pltpu.VMEM((width, 5 * width), BF),
            pltpu.VMEM((4 * width, width), BF),
            pltpu.SemaphoreType.DMA((8,)),
        ],
        compiler_params=params(),
        cost_estimate=cost(18 * rows * width * width, 60 * rows * width),
        name="forward",
    )(att, flat, cot, vec, *mid, *low, *after)


def backward_kernel(gout_ref, res_ref, slope_ref, n1_ref, inv_ref, vec_ref, *refs):
    mid, low = refs[:4], refs[4:8]
    (
        ginner_ref, res1_ref, gbranch_ref, gatt_ref, wide_ref, sum_ref, w1, w2, sem,
    ) = refs[-9:]
    width = gout_ref.shape[1]
    step = pl.program_id(0)
    copies = fetch(mid, w1, sem, 0) + fetch(low, w2, sem, 4)

    @pl.when(step == 0)
    def _():
        for copy in copies:
            copy.start()
        for copy in copies:
            copy.wait()

    gout = gout_ref[...]
    g_first = res_ref[...]
    sums = []
    for f in range(4):
        cut = slice(f * width, (f + 1) * width)
        g_active = dot_nt(gout, w2[cut, :])
        g_inner = (g_active * slope_ref[:, cut]).astype(BF)
        ginner_ref[:, cut] = g_inner
        sums.append(row_sum(g_inner.astype(F32)))
        g_first = g_first + dot_nt(g_inner, w1[:, (f + 1) * width : (f + 2) * width])
    accumulate(wide_ref, sums)
    n1 = n1_ref[...]
    res1 = norm_back(g_first, n1, inv_ref[:, 0:1], vec_ref[3:4, :])
    res1_ref[...] = res1
    g_branch = res1.astype(BF)
    gbranch_ref[...] = g_branch
    gatt_ref[...] = dot_nt(g_branch, w1[:, :width]).astype(BF)
    accumulate(
        sum_ref,
        [row_sum(g_first * n1), row_sum(g_first), row_sum(g_branch.astype(F32))],
    )


def backward(gout, res, slope, n1, inv, vec, mid, low, after):
    rows, width = gout.shape
    block = pl.BlockSpec((BLOCK, width), lambda i: (i, 0))
    wide = pl.BlockSpec((BLOCK, 4 * width), lambda i: (i, 0))
    narrow = pl.BlockSpec((BLOCK, LANES), lambda i: (i, 0))
    sums = pl.BlockSpec((8, width), lambda i: (0, 0))
    s = jax.ShapeDtypeStruct
    return pl.pallas_call(
        backward_kernel,
        grid=(rows // BLOCK,),
        in_specs=[block, block, wide, block, narrow]
        + [once(vec.shape, lambda i: (0, 0))]
        + [ANY] * (8 + len(after)),
        out_specs=(wide, block, block, block, sums, sums),
        out_shape=(
            s((rows, 4 * width), BF),
            s((rows, width), F32),
            s((rows, width), BF),
            s((rows, width), BF),
            s((8, width), F32),
            s((8, width), F32),
        ),
        scratch_shapes=[
            pltpu.VMEM((width, 5 * width), BF),
            pltpu.VMEM((4 * width, width), BF),
            pltpu.SemaphoreType.DMA((8,)),
        ],
        compiler_params=params(),
        cost_estimate=cost(18 * rows * width * width, 50 * rows * width),
        name="backward",
    )(gout, res, slope, n1, inv, vec, *mid, *low, *after)


def outer_grad_kernel(side_ref, far_ref, near_ref, g_ref, *refs):
    send_ref, keep_ref = refs[-2:]
    g = g_ref[...]
    send_ref[...] = dot_tn(far_ref[...], g).astype(BF)
    keep_ref[...] = dot_tn(near_ref[...], g).astype(BF)


def outer_grad(side, active, gout, after):
    rows, width = gout.shape
    columns = active.shape[1]
    tile = width // 2
    steps = columns // 2 // tile
    out = pl.BlockSpec((tile, width), lambda i, s: (i, 0))
    shape = jax.ShapeDtypeStruct((columns // 2, width), BF)
    return pl.pallas_call(
        outer_grad_kernel,
        grid_spec=pltpu.PrefetchScalarGridSpec(
            num_scalar_prefetch=1,
            grid=(steps,),
            in_specs=[
                pl.BlockSpec((rows, tile), lambda i, s: (0, (1 - s[0]) * steps + i)),
                pl.BlockSpec((rows, tile), lambda i, s: (0, s[0] * steps + i)),
                once((rows, width), lambda i, s: (0, 0)),
            ]
            + [ANY] * len(after),
            out_specs=[out, out],
        ),
        out_shape=(shape, shape),
        compiler_params=params(),
        cost_estimate=cost(2 * rows * columns * width, 2 * rows * columns),
        name="outer_grad",
    )(side, active, active, gout, *after)


def inner_grad_kernel(side_ref, af_ref, an_ref, bf_ref, bn_ref, gi_ref, gb_ref, *refs):
    send_ref, keep_ref = refs[-2:]

    @pl.when(pl.program_id(0) == 0)
    def _():
        g = gb_ref[...]
        send_ref[...] = dot_tn(bf_ref[...], g).astype(BF)
        keep_ref[...] = dot_tn(bn_ref[...], g).astype(BF)

    @pl.when(pl.program_id(0) != 0)
    def _():
        g = gi_ref[...]
        send_ref[...] = dot_tn(af_ref[...], g).astype(BF)
        keep_ref[...] = dot_tn(an_ref[...], g).astype(BF)


def inner_grad(side, first, att, g_inner, g_branch, after):
    rows, width = first.shape
    half = width // 2
    near = once((rows, half), lambda i, s: (0, s[0]))
    far = once((rows, half), lambda i, s: (0, 1 - s[0]))
    out = pl.BlockSpec((half, width), lambda i, s: (0, i))
    shape = jax.ShapeDtypeStruct((half, 5 * width), BF)
    return pl.pallas_call(
        inner_grad_kernel,
        grid_spec=pltpu.PrefetchScalarGridSpec(
            num_scalar_prefetch=1,
            grid=(5,),
            in_specs=[far, near, far, near]
            + [
                pl.BlockSpec((rows, width), lambda i, s: (0, jnp.maximum(i - 1, 0))),
                once((rows, width), lambda i, s: (0, 0)),
            ]
            + [ANY] * len(after),
            out_specs=[out, out],
        ),
        out_shape=(shape, shape),
        compiler_params=params(),
        cost_estimate=cost(10 * rows * width * width, 20 * rows * width),
        name="inner_grad",
    )(side, first, first, att, att, g_inner, g_branch, *after)


def input_grad_kernel(side_ref, far_ref, near_ref, g_ref, vf_ref, vn_ref, *refs):
    send_ref, keep_ref = refs[-2:]
    width = g_ref.shape[-1]
    for i in range(3):

        @pl.when(pl.program_id(0) == i)
        def _(i=i):
            g = g_ref[0]
            cut = slice(i * width, (i + 1) * width)
            send_ref[:, cut] = dot_tn(far_ref[...], g).astype(BF)
            keep_ref[:, cut] = dot_tn(near_ref[...], g).astype(BF)

    @pl.when(pl.program_id(0) == 0)
    def _():
        send_ref[:, 3 * width :] = vf_ref[...]
        keep_ref[:, 3 * width :] = vn_ref[...]


def input_grad(side, flat, g, vec, after):
    rows, width = flat.shape
    half = width // 2
    out = once((half, 3 * width + LANES), lambda i, s: (0, 0))
    shape = jax.ShapeDtypeStruct((half, 3 * width + LANES), BF)
    return pl.pallas_call(
        input_grad_kernel,
        grid_spec=pltpu.PrefetchScalarGridSpec(
            num_scalar_prefetch=1,
            grid=(3,),
            in_specs=[
                once((rows, half), lambda i, s: (0, 1 - s[0])),
                once((rows, half), lambda i, s: (0, s[0])),
                pl.BlockSpec((1, rows, width), lambda i, s: (i, 0, 0)),
                once((half, LANES), lambda i, s: (1 - s[0], 0)),
                once((half, LANES), lambda i, s: (s[0], 0)),
            ]
            + [ANY] * len(after),
            out_specs=[out, out],
        ),
        out_shape=(shape, shape),
        compiler_params=params(),
        cost_estimate=cost(6 * rows * width * width, 10 * rows * width),
        name="input_grad",
    )(side, flat, flat, g, vec, vec, *after)


def rows_grad_kernel(g_ref, res_ref, *refs):
    pieces, (low_ref, mem_ref), (w, sem) = refs[:4], refs[-4:-2], refs[-2:]
    width = res_ref.shape[1]

    @pl.when(pl.program_id(0) == 0)
    def _():
        copies = fetch(pieces, w, sem, 0)
        for copy in copies:
            copy.start()
        for copy in copies:
            copy.wait()

    total = res_ref[...]
    for i in range(3):
        total = total + dot_nt(g_ref[i], w[:, i * width : (i + 1) * width])
    low_ref[...] = total.astype(BF)
    mem_ref[0, :MEM] = total[:MEM] + total[SEG - 16 :][16 - MEM :]


def rows_grad(g, res, pieces, after):
    rows, width = res.shape
    columns = pieces[0].shape[1] + pieces[2].shape[1]
    count = rows // SEG
    block = pl.BlockSpec((SEG, width), lambda i: (i, 0))
    return pl.pallas_call(
        rows_grad_kernel,
        grid=(count,),
        in_specs=[pl.BlockSpec((3, SEG, width), lambda i: (0, i, 0)), block]
        + [ANY] * (4 + len(after)),
        out_specs=(block, pl.BlockSpec((1, MEM, width), lambda i: (i, 0, 0))),
        out_shape=(
            jax.ShapeDtypeStruct((rows, width), BF),
            jax.ShapeDtypeStruct((count, MEM, width), F32),
        ),
        scratch_shapes=[
            pltpu.VMEM((width, columns), BF),
            pltpu.SemaphoreType.DMA((4,)),
        ],
        compiler_params=params(),
        cost_estimate=cost(6 * rows * width * width, 12 * rows * width),
        name="rows_grad",
    )(g, res, *pieces, *after)


def columns_of(vectors, rows):
    block = jnp.concatenate([v.reshape(-1, rows).T for v in vectors], axis=1)
    return jnp.pad(block, ((0, 0), (0, LANES - block.shape[1])))


def whole_pieces(w, side, columns):
    near, far = side * (w.shape[0] // 2), (1 - side) * (w.shape[0] // 2)
    cut = [
        lax.dynamic_slice_in_dim(w, at, w.shape[0] // 2, axis=0) for at in (near, far)
    ]
    half = columns // 2 // LANES * LANES
    return cut[0][:, :half], cut[1][:, :half], cut[0][:, half:], cut[1][:, half:]


def per_device(tokens, read_memory, valid_count, cotangent, *parameters):
    side = lax.axis_index("seq")
    ring = lax.axis_size("fsdp") == 16
    p = dict(zip(NAMES, parameters))
    half = tokens.shape[0] // 2
    near = side * half
    far = (1 - side) * half
    width = tokens.shape[2]
    shard = p["Wq"].shape[0]
    side_ref = jnp.full((1,), side, jnp.int32)

    def take(x, at):
        return lax.dynamic_slice_in_dim(x, at, half, axis=0)

    def merge(x):
        own, got = take(x, near), hop_core(take(x, far))
        return jnp.where(side == 0, own, got), jnp.where(side == 0, got, own)

    if ring:
        vectors = [p[n] for n in VECTORS] + [p["b1"]]
        top = jnp.concatenate(
            [p["Wq"], p["Wk"], p["Wv"], columns_of(vectors, shard)], axis=1
        )
        top = gather_group(top)
        mid = gather_group(jnp.concatenate([p["Wo"], p["W1"]], axis=1))
        low = gather_group(p["W2"])
        tail = [t[:, -LANES:] for t in top[2:]]
        block = jnp.concatenate(
            [jnp.where(side == 0, tail[0], tail[1]), jnp.where(side == 0, tail[1], tail[0])]
        )
        vec = block[:, :16].astype(F32).T
        inner = vec[8:12].reshape(4, 32, shard).transpose(1, 0, 2).reshape(4, width)
        vec = jnp.concatenate([vec[:8], inner, vec[12:]])
    else:
        full = {n: lax.all_gather(v, AXES, axis=0, tiled=True) for n, v in p.items()}
        blank = jnp.zeros((width, LANES), BF)
        top = jnp.concatenate([full["Wq"], full["Wk"], full["Wv"], blank], axis=1)
        mid = jnp.concatenate([full["Wo"], full["W1"]], axis=1)
        top, mid, low = (
            whole_pieces(w, side, w.shape[1]) for w in (top, mid, full["W2"])
        )
        vec = jnp.stack([full[n] for n in VECTORS]).astype(F32)
        vec = jnp.concatenate([vec, full["b1"].astype(F32).reshape(4, width)])
        vec = jnp.pad(vec, ((0, 4), (0, 0)))

    mem = take(read_memory, near)
    valid = take(valid_count, near)
    low_tok, high_tok = merge(tokens)
    flat = jnp.concatenate([mem, low_tok, high_tok, mem], axis=1).reshape(-1, width)
    cot = jnp.concatenate(merge(cotangent), axis=1).reshape(-1, width)

    q, k, v = project(flat, vec, top, ())
    att, logs = attend(valid, q, k, v, ())
    out, first, n1, inv1, active, slope, res2, gout, sum2 = forward(
        att, flat, cot, vec, mid, low, ()
    )
    w2_send, w2_keep = outer_grad(side_ref, active, gout, ())
    g_inner, res1, g_branch, g_att, sum_b1, sum1 = backward(
        gout, res2, slope, n1, inv1, vec, mid, low, ()
    )
    w1_send, w1_keep = inner_grad(side_ref, first, att, g_inner, g_branch, ())
    g_qkv, sum_qv = attend_back(valid, q, k, v, g_att, logs, ())
    sum_qv = jnp.sum(sum_qv, axis=0)
    grads = [sum_qv[0], sum_qv[1], sum1[2], sum1[0], sum1[1], sum2[2], sum2[0], sum2[1]]
    if ring:
        b1 = sum_b1[:4].reshape(32, 4, shard).transpose(1, 0, 2).reshape(4, width)
        block = jnp.concatenate([jnp.stack(grads), b1]).astype(BF)
        block = jnp.pad(block.T, ((0, 0), (0, LANES - 12)))
    else:
        block = jnp.zeros((width, LANES), BF)
    top_send, top_keep = input_grad(side_ref, flat, g_qkv, block, ())
    grad_low, grad_mem = rows_grad(g_qkv, res1, top, ())

    shards = {}
    if ring:
        shards["W2"] = scatter_group(w2_send, w2_keep)
        got = scatter_group(w1_send, w1_keep)
        shards["Wo"], shards["W1"] = got[:, :width], got[:, width:]
        got = scatter_group(top_send, top_keep)
        for i, n in enumerate(("Wq", "Wk", "Wv")):
            shards[n] = got[:, i * width : (i + 1) * width]
        got = got[:, 3 * width : 3 * width + 12].T
        for i, n in enumerate(VECTORS):
            shards[n] = got[i]
        shards["b1"] = got[8:12].reshape(-1)
    else:

        def whole(send, keep):
            return jnp.concatenate(
                [jnp.where(side == 0, keep, send), jnp.where(side == 0, send, keep)]
            ).astype(F32)

        full = {"W2": whole(w2_send, w2_keep)}
        got = whole(w1_send, w1_keep)
        full["Wo"], full["W1"] = got[:, :width], got[:, width:]
        got = whole(top_send, top_keep)
        for i, n in enumerate(("Wq", "Wk", "Wv")):
            full[n] = got[:, i * width : (i + 1) * width]
        full.update(zip(VECTORS, grads))
        full["b1"] = sum_b1[:4].reshape(-1)
        shards = {
            n: lax.psum_scatter(g, AXES, scatter_dimension=0, tiled=True)
            for n, g in full.items()
        }

    def back(low, high):
        own = jnp.where(side == 0, low, high)
        got = hop_core(jnp.where(side == 0, high, low))
        return jnp.concatenate(
            [jnp.where(side == 0, own, got), jnp.where(side == 0, got, own)]
        )

    middle = SEG // 2
    out = out.reshape(half, SEG, width)
    layer_out = back(out[:, :middle], out[:, middle:])
    grad_low = grad_low.reshape(half, SEG, width)
    tokens_grad = back(grad_low[:, MEM:middle], grad_low[:, middle : SEG - MEM])
    got = hop_core(grad_mem)
    memory_grad = jnp.concatenate(
        [jnp.where(side == 0, grad_mem, got), jnp.where(side == 0, got, grad_mem)]
    )
    return (layer_out, tokens_grad, memory_grad) + tuple(shards[n] for n in NAMES)


def solution(mesh):
    row = P("fsdp", "seq", None)
    whole = P("fsdp", None, None)
    mat, vec = P(AXES, None), P(AXES)
    specs = tuple(mat if n[0] == "W" else vec for n in NAMES)
    return jax.shard_map(
        per_device,
        mesh=mesh,
        in_specs=(row, whole, P("fsdp"), row) + specs,
        out_specs=(row, row, whole) + specs,
        check_vma=False,
    )
```

```python
import functools
import math

import jax
import jax.numpy as jnp
from jax import lax
from jax.experimental import pallas as pl
from jax.experimental.pallas import tpu as pltpu
from jax.sharding import PartitionSpec as P

HD = 64
MEM = 10
SEG = 512
LANES = 128
BLOCK = 256
BF = jnp.bfloat16
F32 = jnp.float32

EPSILON = 1e-12
ROOT_HALF = math.sqrt(0.5)
INV_ROOT_TAU = 1.0 / math.sqrt(2.0 * math.pi)
AXES = ("seq", "fsdp")
NAMES = ("Wq", "bq", "Wk", "Wv", "bv", "Wo", "bo", "g1", "s1", "W1", "b1", "W2", "b2")
NAMES = NAMES + ("g2", "s2")
VECTORS = ("bq", "bv", "bo", "g1", "s1", "b2", "g2", "s2")
VMEM_LIMIT = 60 * 1024 * 1024

ANY = pl.BlockSpec(memory_space=pl.ANY)


def dot(a, b):
    return jnp.dot(a, b, preferred_element_type=F32)


def dot_nt(a, b):
    return lax.dot_general(a, b, (((1,), (1,)), ((), ())), preferred_element_type=F32)


def dot_tn(a, b):
    return lax.dot_general(a, b, (((0,), (0,)), ((), ())), preferred_element_type=F32)


def cost(flops, moved, transcendentals=0):
    return pl.CostEstimate(
        flops=int(flops),
        bytes_accessed=int(moved),
        transcendentals=int(transcendentals),
    )


def params(**more):
    return pltpu.CompilerParams(vmem_limit_bytes=VMEM_LIMIT, **more)


def once(shape, index):
    return pl.BlockSpec(shape, index, pipeline_mode=pl.Buffered(1))


def hop_z(x):
    size = lax.axis_size("fsdp")
    sends = x if isinstance(x, (list, tuple)) else [x] * 3
    return [
        lax.ppermute(send, "fsdp", [(i, i ^ (4 * d)) for i in range(size)])
        for d, send in enumerate(sends, 1)
    ]


def hop_plane(x, stage):
    size = lax.axis_size("fsdp")
    pairs = []
    for core in range(2):
        bit = 1 << (core ^ stage)
        pairs += [(core * size + i, core * size + (i ^ bit)) for i in range(size)]
    return lax.ppermute(x, AXES, pairs)


def hop_core(x):
    return lax.ppermute(x, "seq", [(0, 1), (1, 0)])


def place():
    me = lax.axis_index("fsdp")
    return me >> 2, (me >> 1) & 1, me & 1


def plane_bits():
    _, yi, xi = place()
    side = lax.axis_index("seq")
    return jnp.where(side == 0, xi, yi), jnp.where(side == 0, yi, xi)


def row_of(z, first, second):
    side = lax.axis_index("seq")
    return z * 4 + jnp.where(side == 0, second * 2 + first, first * 2 + second)


def local(kernel, arrays, shapes, after, name):
    moved = sum(2 * a.size for a in arrays) + sum(2 * math.prod(x) for x in shapes)
    whole = pl.BlockSpec(memory_space=pltpu.VMEM)
    return pl.pallas_call(
        kernel,
        out_shape=tuple(jax.ShapeDtypeStruct(x, BF) for x in shapes),
        in_specs=[whole] * len(arrays) + [ANY] * len(after),
        out_specs=(whole,) * len(shapes),
        compiler_params=params(),
        cost_estimate=cost(0, moved),
        name=name,
    )(*arrays, *after)


def pack_kernel(count, *refs):
    out_ref, at = refs[-1], 0
    for ref in refs[:count]:
        out_ref[:, at : at + ref.shape[1]] = ref[...]
        at += ref.shape[1]


def pack(arrays, after):
    shape = (arrays[0].shape[0], sum(a.shape[1] for a in arrays))
    kernel = functools.partial(pack_kernel, len(arrays))
    return local(kernel, arrays, (shape,), after, "pack")[0]


def merge_z_kernel(x_ref, g1_ref, g2_ref, g3_ref, *refs):
    out_ref = refs[-1]
    zi, _, _ = place()
    for d, ref in enumerate((x_ref, g1_ref, g2_ref, g3_ref)):
        out_ref[pl.ds(jnp.bitwise_xor(zi, d), 1)] = ref[...][None]


def merge_one_kernel(a_ref, g_ref, *refs):
    out_ref = refs[-1]
    bit, _ = plane_bits()
    out_ref[pl.ds(bit, 1)] = a_ref[...][None]
    out_ref[pl.ds(1 - bit, 1)] = g_ref[...][None]


def merge_two_kernel(a_ref, g_ref, *refs):
    out_ref = refs[-1]
    _, bit = plane_bits()
    for ref, second in ((a_ref, bit), (g_ref, 1 - bit)):
        for first in range(2):
            for z in range(4):
                out_ref[pl.ds(row_of(z, first, second), 1)] = ref[first, z][None]


def merge_z(x, g, after):
    return local(merge_z_kernel, [x] + g, ((4,) + x.shape,), after, "merge_z")[0]


def merge_one(a, g, after):
    return local(merge_one_kernel, [a, g], ((2,) + a.shape,), after, "merge_one")[0]


def merge_two(a, g, after):
    rows, columns = a.shape[2:]
    shapes = ((16, rows, columns),)
    out = local(merge_two_kernel, [a, g], shapes, after, "merge_two")[0]
    return out.reshape(16 * rows, columns)


def plus(x, y):
    return (x.astype(F32) + y.astype(F32)).astype(BF)


def split_one_kernel(keep_ref, got_ref, *refs):
    _, bit = plane_bits()
    for ref, second in zip(refs[-2:], (1 - bit, bit)):
        for first in range(2):
            for z in range(4):
                at = pl.ds(row_of(z, first, second), 1)
                ref[first, z] = plus(keep_ref[at], got_ref[at])[0]


def split_two_kernel(keep_ref, got_ref, *refs):
    bit, _ = plane_bits()
    for ref, first in zip(refs[-2:], (1 - bit, bit)):
        at = pl.ds(first, 1)
        ref[...] = plus(keep_ref[at], got_ref[at])[0]


def split_z_kernel(keep_ref, got_ref, *refs):
    zi, _, _ = place()
    for d, ref in enumerate(refs[-4:]):
        at = pl.ds(jnp.bitwise_xor(zi, d), 1)
        ref[...] = plus(keep_ref[at], got_ref[at])[0]


def split_one(keep, got, after):
    columns = keep.shape[1]
    keep, got = (x.reshape(16, -1, columns) for x in (keep, got))
    shape = (2, 4) + keep.shape[1:]
    return local(split_one_kernel, [keep, got], (shape,) * 2, after, "split_one")


def split_two(keep, got, after):
    shape = keep.shape[1:]
    return local(split_two_kernel, [keep, got], (shape,) * 2, after, "split_two")


def split_z(keep, got, after):
    shape = keep.shape[1:]
    return local(split_z_kernel, [keep, got], (shape,) * 4, after, "split_z")


def total_of(keep, got):
    total = keep.astype(F32)
    for term in got:
        total = total + term.astype(F32)
    return total


class Fetch:
    def __init__(self, pieces, target, sem, at, chunks, by_rows):
        self.pieces, self.target, self.sem, self.at = pieces, target, sem, at
        self.chunks, self.by_rows = chunks, by_rows
        self.side = lax.axis_index("seq")

    def copy(self, chunk, piece):
        source, slot = self.pieces[piece], self.at + chunk
        height, width = self.target.shape
        if self.by_rows:
            rows = height // self.chunks
            local = chunk % (self.chunks // 2) * rows
            return pltpu.make_async_copy(
                source.at[pl.ds(local, rows)],
                self.target.at[pl.ds(chunk * rows, rows)],
                self.sem.at[slot],
            )
        columns = width // self.chunks // LANES * LANES
        end = width if chunk == self.chunks - 1 else (chunk + 1) * columns
        cut = slice(chunk * columns, end)
        if len(self.pieces) == 1:
            return pltpu.make_async_copy(
                source.at[:, cut], self.target.at[:, cut], self.sem.at[slot]
            )
        core = self.side if piece == 0 else 1 - self.side
        start = pl.multiple_of(core * (height // 2), 16)
        return pltpu.make_async_copy(
            source.at[:, cut],
            self.target.at[pl.ds(start, height // 2), cut],
            self.sem.at[slot + piece * self.chunks],
        )

    def start(self, chunk):
        if not self.by_rows:
            for piece in range(len(self.pieces)):
                self.copy(chunk, piece).start()
            return
        core = chunk // (self.chunks // 2)

        @pl.when(self.side == core)
        def _():
            self.copy(chunk, 0).start()

        @pl.when(self.side != core)
        def _():
            self.copy(chunk, 1).start()

    def wait(self, chunk):
        for piece in range(1 if self.by_rows else len(self.pieces)):
            self.copy(chunk, piece).wait()


def in_steps(body, *copies):
    @pl.when(pl.program_id(0) == 0)
    def _():
        for fetch, chunk in copies:
            fetch.start(chunk)
        body(True)

    @pl.when(pl.program_id(0) != 0)
    def _():
        body(False)


def project_kernel(x_ref, bias_ref, *refs):
    pieces, (q_ref, k_ref, v_ref), (w, sem) = refs[:2], refs[-5:-2], refs[-2:]
    width = x_ref.shape[1]
    fetch = Fetch(pieces, w, sem, 0, 3, False)

    def body(first):
        x = x_ref[...]
        if first:
            fetch.wait(0)
        q = (dot(x, w[:, :width]) + bias_ref[0:1, :]).astype(BF)
        q_ref[...] = (q.astype(F32) * HD ** (-0.5)).astype(BF)
        if first:
            fetch.wait(1)
        k_ref[...] = dot(x, w[:, width : 2 * width]).astype(BF)
        if first:
            fetch.wait(2)
        v = dot(x, w[:, 2 * width : 3 * width]) + bias_ref[1:2, :]
        v_ref[...] = v.astype(BF)

    in_steps(body, *[(fetch, i) for i in range(3)])


def project(flat, bias, pieces, after):
    rows, width = flat.shape
    columns = pieces[0].shape[1]
    block = pl.BlockSpec((BLOCK, width), lambda i: (i, 0))
    out = jax.ShapeDtypeStruct(flat.shape, BF)
    return pl.pallas_call(
        project_kernel,
        grid=(rows // BLOCK,),
        out_shape=(out,) * 3,
        in_specs=[block, once(bias.shape, lambda i: (0, 0))] + [ANY] * (2 + len(after)),
        out_specs=(block,) * 3,
        scratch_shapes=[
            pltpu.VMEM((width, columns), BF),
            pltpu.SemaphoreType.DMA((6,)),
        ],
        compiler_params=params(),
        cost_estimate=cost(6 * rows * width * width, 20 * rows * width),
        name="project",
    )(flat, bias, *pieces, *after)


def lane_masks(rows):
    lane = lax.broadcasted_iota(jnp.int32, (rows, LANES), 1)
    return [lane < HD, lane >= HD]


def key_bias(valid):
    at = lax.broadcasted_iota(jnp.int32, (SEG, 1), 0)
    keep = (at < MEM) | (at >= SEG - MEM) | (at - MEM < valid)
    return jnp.where(keep, 0.0, -1000000000.0)


def attend_kernel(segment, valid_ref, q_ref, k_ref, v_ref, *refs):
    o_ref, log_ref = refs[-2:]
    bias = key_bias(valid_ref[segment]).astype(BF)
    q, k, v = q_ref[...], k_ref[...], v_ref[...]
    lane = lax.broadcasted_iota(jnp.int32, (SEG, LANES), 1)
    heads = q.shape[1] // HD

    def score(h):
        at = slice(h // 2 * LANES, (h // 2 + 1) * LANES)
        mask = (lane < HD) == (h % 2 == 0)
        spare = lane == (1 - h % 2) * HD
        return dot_nt(
            jnp.where(mask, k[:, at], jnp.where(spare, bias, 0)),
            jnp.where(mask, q[:, at], jnp.where(spare, 1, 0).astype(BF)),
        )

    vt = v.T
    outs = []
    ahead = score(0)
    for h in range(heads):
        scores = ahead
        if h + 1 < heads:
            ahead = score(h + 1)
        top = jnp.max(scores, axis=0, keepdims=True)
        weights = jnp.exp(scores - top)
        total = jnp.sum(weights, axis=0, keepdims=True)
        mixed = dot(vt[h * HD : (h + 1) * HD], weights.astype(BF))
        outs.append(mixed * (1.0 / total))
        log_ref[h // 2, h % 2 : h % 2 + 1, :] = top + jnp.log(total)
    o_ref[...] = jnp.concatenate(outs, axis=0).T.astype(BF)


def attend(segment, valid, q, k, v, earlier, after):
    rows, width = q.shape
    count, pairs = rows // SEG, width // LANES
    block = pl.BlockSpec((SEG, 2 * LANES), lambda p, _: (segment, p))
    return pl.pallas_call(
        functools.partial(attend_kernel, segment),
        grid_spec=pltpu.PrefetchScalarGridSpec(
            num_scalar_prefetch=1,
            grid=(pairs // 2,),
            in_specs=[block] * 3 + [ANY] * (len(earlier) + len(after)),
            out_specs=[
                block,
                pl.BlockSpec((2, 8, SEG), lambda p, _: (segment * pairs // 2 + p, 0, 0)),
            ],
        ),
        out_shape=(
            jax.ShapeDtypeStruct(q.shape, BF),
            jax.ShapeDtypeStruct((count * pairs, 8, SEG), F32),
        ),
        input_output_aliases={4 + i: i for i in range(len(earlier))},
        compiler_params=params(),
        cost_estimate=cost(16 * SEG * SEG * width, 8 * SEG * width),
        name="attend",
    )(valid, q, k, v, *earlier, *after)


def attend_back_kernel(segment, valid_ref, q_ref, k_ref, v_ref, g_ref, log_ref, *refs):
    out_ref, sum_ref = refs[-2:]
    bias = key_bias(valid_ref[segment]).astype(BF)
    q, k, v, g = q_ref[...], k_ref[...], v_ref[...], g_ref[...]
    lane = lax.broadcasted_iota(jnp.int32, (SEG, LANES), 1)
    left = lane < HD
    heads = q.shape[1] // HD

    def start(h):
        at = slice(h // 2 * LANES, (h // 2 + 1) * LANES)
        mask = left == (h % 2 == 0)
        spare = lane == (1 - h % 2) * HD
        scores = dot_nt(
            jnp.where(mask, k[:, at], jnp.where(spare, bias, 0)),
            jnp.where(mask, q[:, at], jnp.where(spare, 1, 0).astype(BF)),
        )
        return scores, dot_nt(v[:, at], jnp.where(mask, g[:, at], 0))

    gq, gk, gv = [], [], []
    ahead = start(0)
    for h in range(heads):
        scores, g_probs = ahead
        if h + 1 < heads:
            ahead = start(h + 1)
        at = slice(h // 2 * LANES, (h // 2 + 1) * LANES)
        probs = jnp.exp(scores - log_ref[h // 2, h % 2 : h % 2 + 1, :])
        delta = jnp.sum(probs * g_probs, axis=0, keepdims=True)
        g_scores = (probs * (g_probs - delta)).astype(BF)
        gv.append(dot(probs.astype(BF), g[:, at]))
        gk.append(dot(g_scores, q[:, at]))
        gq.append(dot_tn(g_scores, k[:, at]))

    def both(parts, scale=1.0):
        pairs = range(0, heads, 2)
        return jnp.concatenate(
            [jnp.where(left, parts[i], parts[i + 1]) * scale for i in pairs], axis=1
        ).astype(BF)

    gq, gk, gv = both(gq, HD ** (-0.5)), both(gk), both(gv)
    out_ref[0], out_ref[1], out_ref[2] = gq, gk, gv
    sum_ref[...] = jnp.concatenate(
        [row_sum(gq.astype(F32)), row_sum(gv.astype(F32)), jnp.zeros((6, gq.shape[1]), F32)]
    )[None]


def attend_back(segment, valid, q, k, v, g, logs, earlier, after):
    rows, width = q.shape
    count, pairs = rows // SEG, width // LANES
    block = pl.BlockSpec((SEG, 2 * LANES), lambda p, _: (segment, p))
    return pl.pallas_call(
        functools.partial(attend_back_kernel, segment),
        grid_spec=pltpu.PrefetchScalarGridSpec(
            num_scalar_prefetch=1,
            grid=(pairs // 2,),
            in_specs=[block] * 4
            + [pl.BlockSpec((2, 8, SEG), lambda p, _: (segment * pairs // 2 + p, 0, 0))]
            + [ANY] * (len(earlier) + len(after)),
            out_specs=[
                pl.BlockSpec((3, SEG, 2 * LANES), lambda p, _: (0, segment, p)),
                pl.BlockSpec((1, 8, 2 * LANES), lambda p, _: (segment, 0, p)),
            ],
        ),
        out_shape=(
            jax.ShapeDtypeStruct((3,) + q.shape, BF),
            jax.ShapeDtypeStruct((count, 8, width), F32),
        ),
        input_output_aliases={6 + i: i for i in range(len(earlier))},
        compiler_params=params(),
        cost_estimate=cost(20 * SEG * SEG * width, 14 * SEG * width),
        name="attend_back",
    )(valid, q, k, v, g, logs, *earlier, *after)


def normalize(resid):
    centre = resid - jnp.mean(resid, axis=-1, keepdims=True)
    inverse = lax.rsqrt(jnp.mean(centre * centre, axis=-1, keepdims=True) + EPSILON)
    return centre * inverse, inverse


def norm_back(grad_out, normed, inverse, gain):
    scaled = grad_out * gain
    return inverse * (
        scaled
        - jnp.mean(scaled, axis=-1, keepdims=True)
        - normed * jnp.mean(scaled * normed, axis=-1, keepdims=True)
    )


def gelu_parts(inner):
    phi = 0.5 * (1.0 + lax.erf(inner * ROOT_HALF))
    slope = phi + inner * (jnp.exp(-0.5 * inner * inner) * INV_ROOT_TAU)
    return inner * phi, slope


def row_sum(x):
    return jnp.sum(x, axis=0, keepdims=True)


def accumulate(ref, rows, first):
    stack = jnp.concatenate(
        rows + [jnp.zeros((8 - len(rows), rows[0].shape[1]), F32)], axis=0
    )
    ref[...] = stack if first else ref[...] + stack


def expand_kernel(att_ref, x_ref, vec_ref, *refs):
    mid = refs[:1]
    first_ref, n1_ref, inv_ref, act_ref, slope_ref, w1, sem = refs[-7:]
    width = x_ref.shape[1]
    fetch = Fetch(mid, w1, sem, 0, 5, False)
    vec = lambda i: vec_ref[i : i + 1, :]

    def body(first):
        if first:
            fetch.wait(0)
        branch = dot(att_ref[...], w1[:, :width]) + vec(2)
        n1, inv1 = normalize(x_ref[...].astype(F32) + branch)
        first_low = (n1 * vec(3) + vec(4)).astype(BF)
        n1_ref[...] = n1
        inv_ref[...] = jnp.broadcast_to(inv1, inv_ref.shape)
        first_ref[...] = first_low
        for f in range(4):
            cut = slice(f * width, (f + 1) * width)
            if first:
                fetch.wait(f + 1)
            inner = dot(first_low, w1[:, (f + 1) * width : (f + 2) * width]) + vec(8 + f)
            active, slope = gelu_parts(inner)
            act_ref[:, cut] = active.astype(BF)
            slope_ref[:, cut] = slope.astype(BF)

    in_steps(body, *[(fetch, i) for i in range(5)])


def expand(att, flat, vec, mid, after):
    rows, width = flat.shape
    block = pl.BlockSpec((BLOCK, width), lambda i: (i, 0))
    wide = pl.BlockSpec((BLOCK, 4 * width), lambda i: (i, 0))
    narrow = pl.BlockSpec((BLOCK, LANES), lambda i: (i, 0))
    s = jax.ShapeDtypeStruct
    return pl.pallas_call(
        expand_kernel,
        grid=(rows // BLOCK,),
        in_specs=[block] * 2
        + [once(vec.shape, lambda i: (0, 0))]
        + [ANY] * (1 + len(after)),
        out_specs=(block, block, narrow, wide, wide),
        out_shape=(
            s((rows, width), BF),
            s((rows, width), F32),
            s((rows, LANES), F32),
            s((rows, 4 * width), BF),
            s((rows, 4 * width), BF),
        ),
        scratch_shapes=[
            pltpu.VMEM((width, 5 * width), BF),
            pltpu.SemaphoreType.DMA((6,)),
        ],
        compiler_params=params(),
        cost_estimate=cost(10 * rows * width * width, 40 * rows * width),
        name="expand",
    )(att, flat, vec, *mid, *after)


def contract_kernel(act_ref, n1_ref, cot_ref, vec_ref, *refs):
    low = refs[:2]
    out_ref, res_ref, gout_ref, sum_ref, w2, sem = refs[-6:]
    width = n1_ref.shape[1]
    fetch = Fetch(low, w2, sem, 0, 4, True)
    vec = lambda i: vec_ref[i : i + 1, :]

    def body(first_step):
        if first_step:
            outer = vec(5)
            for f in range(4):
                cut = slice(f * width, (f + 1) * width)
                fetch.wait(f)
                outer = outer + dot(act_ref[:, cut], w2[cut, :])
        else:
            outer = dot(act_ref[...], w2[...]) + vec(5)
        first = n1_ref[...] * vec(3) + vec(4)
        n2, inv2 = normalize(first + outer)
        out_ref[...] = (n2 * vec(6) + vec(7)).astype(BF)
        cot = cot_ref[...].astype(F32)
        res = norm_back(cot, n2, inv2, vec(6))
        res_ref[...] = res
        gout = res.astype(BF)
        gout_ref[...] = gout
        sums = [row_sum(cot * n2), row_sum(cot), row_sum(gout.astype(F32))]
        accumulate(sum_ref, sums, first_step)

    in_steps(body, *[(fetch, i) for i in range(4)])


def contract(active, n1, cot, vec, low, after):
    rows, width = n1.shape
    block = pl.BlockSpec((BLOCK, width), lambda i: (i, 0))
    wide = pl.BlockSpec((BLOCK, 4 * width), lambda i: (i, 0))
    s = jax.ShapeDtypeStruct
    return pl.pallas_call(
        contract_kernel,
        grid=(rows // BLOCK,),
        in_specs=[wide, block, block]
        + [once(vec.shape, lambda i: (0, 0))]
        + [ANY] * (2 + len(after)),
        out_specs=(block, block, block, pl.BlockSpec((8, width), lambda i: (0, 0))),
        out_shape=(
            s((rows, width), BF),
            s((rows, width), F32),
            s((rows, width), BF),
            s((8, width), F32),
        ),
        scratch_shapes=[
            pltpu.VMEM((4 * width, width), BF),
            pltpu.SemaphoreType.DMA((9,)),
        ],
        compiler_params=params(),
        cost_estimate=cost(8 * rows * width * width, 24 * rows * width),
        name="contract",
    )(active, n1, cot, vec, *low, *after)


def backward_kernel(gout_ref, res_ref, slope_ref, n1_ref, inv_ref, vec_ref, *refs):
    mid, low = refs[:1], refs[1:3]
    (
        ginner_ref, res1_ref, gbranch_ref, gatt_ref, wide_ref, sum_ref, w1, w2, sem,
    ) = refs[-9:]
    width = gout_ref.shape[1]
    up = Fetch(mid, w1, sem, 0, 5, False)
    down = Fetch(low, w2, sem, 5, 4, True)
    copies = []
    for f in range(4):
        copies += [(down, f), (up, f + 1)]

    def body(first):
        def slopes(f):
            if first:
                down.wait(f)
            return dot_nt(gout, w2[f * width : (f + 1) * width, :])

        gout = gout_ref[...]
        g_first = res_ref[...]
        sums = []
        for f in range(4):
            cut = slice(f * width, (f + 1) * width)
            g_active = slopes(f)
            g_inner = (g_active * slope_ref[:, cut].astype(F32)).astype(BF)
            ginner_ref[:, cut] = g_inner
            sums.append(row_sum(g_inner.astype(F32)))
            if first:
                up.wait(f + 1)
            g_first = g_first + dot_nt(g_inner, w1[:, (f + 1) * width : (f + 2) * width])
        accumulate(wide_ref, sums, first)
        n1 = n1_ref[...]
        res1 = norm_back(g_first, n1, inv_ref[:, 0:1], vec_ref[3:4, :])
        res1_ref[...] = res1
        g_branch = res1.astype(BF)
        gbranch_ref[...] = g_branch
        if first:
            up.wait(0)
        gatt_ref[...] = dot_nt(g_branch, w1[:, :width]).astype(BF)
        sums = [row_sum(g_first * n1), row_sum(g_first), row_sum(g_branch.astype(F32))]
        accumulate(sum_ref, sums, first)

    in_steps(body, *copies, (up, 0))


def backward(gout, res, slope, n1, inv, vec, mid, low, after):
    rows, width = gout.shape
    block = pl.BlockSpec((BLOCK, width), lambda i: (i, 0))
    wide = pl.BlockSpec((BLOCK, 4 * width), lambda i: (i, 0))
    narrow = pl.BlockSpec((BLOCK, LANES), lambda i: (i, 0))
    sums = pl.BlockSpec((8, width), lambda i: (0, 0))
    s = jax.ShapeDtypeStruct
    return pl.pallas_call(
        backward_kernel,
        grid=(rows // BLOCK,),
        in_specs=[block, block, wide, block, narrow]
        + [once(vec.shape, lambda i: (0, 0))]
        + [ANY] * (3 + len(after)),
        out_specs=(wide, block, block, block, sums, sums),
        out_shape=(
            s((rows, 4 * width), BF),
            s((rows, width), F32),
            s((rows, width), BF),
            s((rows, width), BF),
            s((8, width), F32),
            s((8, width), F32),
        ),
        scratch_shapes=[
            pltpu.VMEM((width, 5 * width), BF),
            pltpu.VMEM((4 * width, width), BF),
            pltpu.SemaphoreType.DMA((9,)),
        ],
        compiler_params=params(),
        cost_estimate=cost(18 * rows * width * width, 50 * rows * width),
        name="backward",
    )(gout, res, slope, n1, inv, vec, *mid, *low, *after)


def outer_grad_kernel(side_ref, far_ref, near_ref, g_ref, send_ref, keep_ref):
    g = g_ref[...]
    send_ref[...] = dot_tn(far_ref[...], g).astype(BF)
    keep_ref[...] = dot_tn(near_ref[...], g).astype(BF)


def outer_grad(side, active, gout):
    rows, width = gout.shape
    columns = active.shape[1]
    steps = columns // 2 // width
    out = pl.BlockSpec((width, width), lambda i, s: (i, 0))
    shape = jax.ShapeDtypeStruct((columns // 2, width), BF)
    return pl.pallas_call(
        outer_grad_kernel,
        grid_spec=pltpu.PrefetchScalarGridSpec(
            num_scalar_prefetch=1,
            grid=(steps,),
            in_specs=[
                pl.BlockSpec((rows, width), lambda i, s: (0, (1 - s[0]) * steps + i)),
                pl.BlockSpec((rows, width), lambda i, s: (0, s[0] * steps + i)),
                once((rows, width), lambda i, s: (0, 0)),
            ],
            out_specs=[out, out],
        ),
        out_shape=(shape, shape),
        compiler_params=params(),
        cost_estimate=cost(2 * rows * columns * width, 2 * rows * columns),
        name="outer_grad",
    )(side, active, active, gout)


def inner_grad_kernel(a_ref, b_ref, gi_ref, gb_ref, *refs):
    out_ref = refs[-1]

    @pl.when(pl.program_id(0) == 0)
    def _():
        out_ref[...] = dot_tn(b_ref[...], gb_ref[...]).astype(BF)

    @pl.when(pl.program_id(0) != 0)
    def _():
        out_ref[...] = dot_tn(a_ref[...], gi_ref[...]).astype(BF)


def inner_grad(first, att, g_inner, g_branch, after):
    rows, width = first.shape
    whole = once((rows, width), lambda i: (0, 0))
    return pl.pallas_call(
        inner_grad_kernel,
        grid=(5,),
        in_specs=[
            whole,
            whole,
            pl.BlockSpec((rows, width), lambda i: (0, jnp.maximum(i - 1, 0))),
            whole,
        ]
        + [ANY] * len(after),
        out_specs=pl.BlockSpec((width, width), lambda i: (0, i)),
        out_shape=jax.ShapeDtypeStruct((width, 5 * width), BF),
        compiler_params=params(),
        cost_estimate=cost(10 * rows * width * width, 20 * rows * width),
        name="inner_grad",
    )(first, att, g_inner, g_branch, *after)


def input_grad_kernel(side_ref, far_ref, near_ref, g_ref, vf_ref, vn_ref, *refs):
    send_ref, keep_ref = refs[-2:]
    width = g_ref.shape[-1]
    for i in range(3):

        @pl.when(pl.program_id(0) == i)
        def _(i=i):
            g = g_ref[0]
            cut = slice(i * width, (i + 1) * width)
            send_ref[:, cut] = dot_tn(far_ref[...], g).astype(BF)
            keep_ref[:, cut] = dot_tn(near_ref[...], g).astype(BF)

    @pl.when(pl.program_id(0) == 0)
    def _():
        send_ref[:, 3 * width :] = vf_ref[...]
        keep_ref[:, 3 * width :] = vn_ref[...]


def input_grad(side, flat, g, vec, after):
    rows, width = flat.shape
    half = width // 2
    out = once((half, 3 * width + LANES), lambda i, s: (0, 0))
    shape = jax.ShapeDtypeStruct((half, 3 * width + LANES), BF)
    return pl.pallas_call(
        input_grad_kernel,
        grid_spec=pltpu.PrefetchScalarGridSpec(
            num_scalar_prefetch=1,
            grid=(3,),
            in_specs=[
                once((rows, half), lambda i, s: (0, 1 - s[0])),
                once((rows, half), lambda i, s: (0, s[0])),
                pl.BlockSpec((1, rows, width), lambda i, s: (i, 0, 0)),
                once((half, LANES), lambda i, s: (1 - s[0], 0)),
                once((half, LANES), lambda i, s: (s[0], 0)),
            ]
            + [ANY] * len(after),
            out_specs=[out, out],
        ),
        out_shape=(shape, shape),
        compiler_params=params(),
        cost_estimate=cost(6 * rows * width * width, 10 * rows * width),
        name="input_grad",
    )(side, flat, flat, g, vec, vec, *after)


def rows_grad_kernel(g_ref, res_ref, *refs):
    pieces, (low_ref, mem_ref), (w, sem) = refs[:2], refs[-4:-2], refs[-2:]
    width = res_ref.shape[1]
    fetch = Fetch(pieces, w, sem, 0, 3, False)

    def body(first):
        total = res_ref[...]
        for i in range(3):
            if first:
                fetch.wait(i)
            total = total + dot_nt(g_ref[i], w[:, i * width : (i + 1) * width])
        low_ref[...] = total.astype(BF)
        mem_ref[0, :MEM] = total[:MEM] + total[SEG - 16 :][16 - MEM :]

    in_steps(body, *[(fetch, i) for i in range(3)])


def rows_grad(g, res, pieces, after):
    rows, width = res.shape
    columns = pieces[0].shape[1]
    count = rows // SEG
    block = pl.BlockSpec((SEG, width), lambda i: (i, 0))
    return pl.pallas_call(
        rows_grad_kernel,
        grid=(count,),
        in_specs=[pl.BlockSpec((3, SEG, width), lambda i: (0, i, 0)), block]
        + [ANY] * (2 + len(after)),
        out_specs=(block, pl.BlockSpec((1, MEM, width), lambda i: (i, 0, 0))),
        out_shape=(
            jax.ShapeDtypeStruct((rows, width), BF),
            jax.ShapeDtypeStruct((count, MEM, width), F32),
        ),
        scratch_shapes=[
            pltpu.VMEM((width, columns), BF),
            pltpu.SemaphoreType.DMA((6,)),
        ],
        compiler_params=params(),
        cost_estimate=cost(6 * rows * width * width, 12 * rows * width),
        name="rows_grad",
    )(g, res, *pieces, *after)


def columns_of(vectors, rows):
    block = jnp.concatenate([jnp.stack(vectors[:-1]), vectors[-1].reshape(-1, rows)])
    return jnp.pad(block, ((0, LANES - block.shape[0]), (0, 0))).T


def whole_pieces(w, side):
    near, far = side * (w.shape[0] // 2), (1 - side) * (w.shape[0] // 2)
    cut = [
        lax.dynamic_slice_in_dim(w, at, w.shape[0] // 2, axis=0) for at in (near, far)
    ]
    return tuple(cut)


def per_device(tokens, read_memory, valid_count, cotangent, *parameters):
    side = lax.axis_index("seq")
    ring = lax.axis_size("fsdp") == 16
    p = dict(zip(NAMES, parameters))
    half = tokens.shape[0] // 2
    near = side * half
    far = (1 - side) * half
    width = tokens.shape[2]
    shard = p["Wq"].shape[0]
    side_ref = jnp.full((1,), side, jnp.int32)

    def take(x, at):
        return lax.dynamic_slice_in_dim(x, at, half, axis=0)

    def merge(x):
        own, got = take(x, near), hop_core(take(x, far))
        return jnp.where(side == 0, own, got), jnp.where(side == 0, got, own)

    mem = take(read_memory, near)
    valid = take(valid_count, near)
    low_tok, high_tok = merge(tokens)
    flat = jnp.concatenate([mem, low_tok, high_tok, mem], axis=1).reshape(-1, width)
    cot = jnp.concatenate(merge(cotangent), axis=1).reshape(-1, width)

    mid = pack([p["Wo"], p["W1"]], ())
    mid_shard = mid
    mid = (lax.all_gather(mid, AXES, axis=0, tiled=True),)
    if ring:
        vectors = columns_of([p[n] for n in VECTORS] + [p["b1"]], shard)
        top = pack([p["Wq"], p["Wk"], p["Wv"], vectors], [mid_shard])
        t = merge_z(top, hop_z(top), ())
        got = hop_plane(t, 0)
        low = pack([p["W2"]], [t])
        t = merge_one(t, got, [low, flat])
        low_z = hop_z(low)
        own = merge_two(t, hop_plane(t, 1), [*low_z, cot])
        top = (own, hop_core(own))
        tail = [t[:, -LANES:] for t in top]
        block = jnp.concatenate(
            [jnp.where(side == 0, tail[0], tail[1]), jnp.where(side == 0, tail[1], tail[0])]
        )
        vec = block[:, :16].astype(F32).T
        inner = vec[8:12].reshape(4, 32, shard).transpose(1, 0, 2).reshape(4, width)
        vec = jnp.concatenate([vec[:8], inner, vec[12:]])
    else:
        full = {
            n: lax.all_gather(v, AXES, axis=0, tiled=True)
            for n, v in p.items()
            if n not in ("Wo", "W1")
        }
        blank = jnp.zeros((width, LANES), BF)
        top = jnp.concatenate([full["Wq"], full["Wk"], full["Wv"], blank], axis=1)
        top, low = (whole_pieces(w, side) for w in (top, full["W2"]))
        vec = jnp.stack([full[n] for n in VECTORS]).astype(F32)
        vec = jnp.concatenate([vec, full["b1"].astype(F32).reshape(4, width)])
        vec = jnp.pad(vec, ((0, 4), (0, 0)))

    if ring:
        t = merge_z(low, low_z, [own])
        got = hop_plane(t, 0)
        q, k, v = project(flat, vec, top, [t])
        t = merge_one(t, got, [v])
        got = hop_plane(t, 1)
        first_half = attend(0, valid, q, k, v, (), [t])
        att, logs = attend(1, valid, q, k, v, first_half, [])
        own = merge_two(t, got, [logs])
        low = (own, hop_core(own))
    else:
        q, k, v = project(flat, vec, top, ())
        first_half = attend(0, valid, q, k, v, (), ())
        att, logs = attend(1, valid, q, k, v, first_half, ())
        own = logs
    first, n1, inv1, active, slope = expand(att, flat, vec, mid, [own])
    out, res2, gout, sum2 = contract(active, n1, cot, vec, low, ())
    send, keep = outer_grad(side_ref, active, gout)
    if ring:
        got = hop_core(send)
    g_inner, res1, g_branch, g_att, sum_b1, sum1 = backward(
        gout, res2, slope, n1, inv1, vec, mid, low, [keep]
    )
    if ring:
        w1_grad = inner_grad(first, att, g_inner, g_branch, ())
        w1_shard = lax.psum_scatter(w1_grad, AXES, scatter_dimension=0, tiled=True)
        send, keep = split_one(keep, got, [w1_grad])
        got = hop_plane(send, 1)
        done = attend_back(0, valid, q, k, v, g_att, logs, (), [send])
        send, keep = split_two(keep, got, [done[1]])
        got = hop_plane(send, 0)
        g_qkv, sum_qv = attend_back(1, valid, q, k, v, g_att, logs, done, [send])
        w2_keep, *sends = split_z(keep, got, [sum_qv])
        w2_z = hop_z(sends)
    else:
        w1_grad = inner_grad(first, att, g_inner, g_branch, [])
        w1_shard = lax.psum_scatter(w1_grad, AXES, scatter_dimension=0, tiled=True)
        done = attend_back(0, valid, q, k, v, g_att, logs, (), ())
        g_qkv, sum_qv = attend_back(1, valid, q, k, v, g_att, logs, done, ())
        w2_keep = keep
    sum_qv = jnp.sum(sum_qv, axis=0)
    grads = [sum_qv[0], sum_qv[1], sum1[2], sum1[0], sum1[1], sum2[2], sum2[0], sum2[1]]
    if ring:
        b1 = sum_b1[:4].reshape(32, 4, shard).transpose(1, 0, 2).reshape(4, width)
        block = jnp.concatenate([jnp.stack(grads), b1]).astype(BF)
        block = jnp.pad(block, ((0, LANES - 12), (0, 0))).T
    else:
        block = jnp.zeros((width, LANES), BF)
    top_send, top_keep = input_grad(side_ref, flat, g_qkv, block, [w2_keep])

    shards = {}
    if ring:
        got = hop_core(top_send)
        grad_low, grad_mem = rows_grad(g_qkv, res1, top, [top_keep])
        top_send, top_keep = split_one(top_keep, got, [grad_mem])
        got = hop_plane(top_send, 1)
        top_send, top_keep = split_two(top_keep, got, w2_z)
        got = hop_plane(top_send, 0)
        top_keep, *sends = split_z(top_keep, got, ())
        shards["W2"] = total_of(w2_keep, w2_z)
        got = total_of(top_keep, hop_z(sends))
        for i, n in enumerate(("Wq", "Wk", "Wv")):
            shards[n] = got[:, i * width : (i + 1) * width]
        got = got[:, 3 * width : 3 * width + 12].T
        for i, n in enumerate(VECTORS):
            shards[n] = got[i]
        shards["b1"] = got[8:12].reshape(-1)
    else:
        grad_low, grad_mem = rows_grad(g_qkv, res1, top, [top_keep])

        def whole(send, keep):
            return jnp.concatenate(
                [jnp.where(side == 0, keep, send), jnp.where(side == 0, send, keep)]
            ).astype(F32)

        full = {"W2": whole(send, keep)}
        got = whole(top_send, top_keep)
        for i, n in enumerate(("Wq", "Wk", "Wv")):
            full[n] = got[:, i * width : (i + 1) * width]
        full.update(zip(VECTORS, grads))
        full["b1"] = sum_b1[:4].reshape(-1)
        for n, g in full.items():
            shards[n] = lax.psum_scatter(g, AXES, scatter_dimension=0, tiled=True)
    w1_shard = w1_shard.astype(F32)
    shards["Wo"], shards["W1"] = w1_shard[:, :width], w1_shard[:, width:]

    def back(low, high):
        own = jnp.where(side == 0, low, high)
        got = hop_core(jnp.where(side == 0, high, low))
        return jnp.concatenate(
            [jnp.where(side == 0, own, got), jnp.where(side == 0, got, own)]
        )

    middle = SEG // 2
    out = out.reshape(half, SEG, width)
    layer_out = back(out[:, :middle], out[:, middle:])
    grad_low = grad_low.reshape(half, SEG, width)
    tokens_grad = back(grad_low[:, MEM:middle], grad_low[:, middle : SEG - MEM])
    got = hop_core(grad_mem)
    memory_grad = jnp.concatenate(
        [jnp.where(side == 0, grad_mem, got), jnp.where(side == 0, got, grad_mem)]
    )
    return (layer_out, tokens_grad, memory_grad) + tuple(shards[n] for n in NAMES)


def solution(mesh):
    row = P("fsdp", "seq", None)
    whole = P("fsdp", None, None)
    mat, vec = P(AXES, None), P(AXES)
    specs = tuple(mat if n[0] == "W" else vec for n in NAMES)
    return jax.shard_map(
        per_device,
        mesh=mesh,
        in_specs=(row, whole, P("fsdp"), row) + specs,
        out_specs=(row, row, whole) + specs,
        check_vma=False,
    )
```

```python
import functools
import math

import jax
import jax.numpy as jnp
from jax import lax
from jax.experimental import pallas as pl
from jax.experimental.pallas import tpu as pltpu
from jax.sharding import PartitionSpec as P

HD = 64
MEM = 10
SEG = 512
LANES = 128
BLOCK = 256
BF = jnp.bfloat16
F32 = jnp.float32

EPSILON = 1e-12
ROOT_HALF = math.sqrt(0.5)
INV_ROOT_TAU = 1.0 / math.sqrt(2.0 * math.pi)
AXES = ("seq", "fsdp")
NAMES = ("Wq", "bq", "Wk", "Wv", "bv", "Wo", "bo", "g1", "s1", "W1", "b1", "W2", "b2")
NAMES = NAMES + ("g2", "s2")
VECTORS = ("bq", "bv", "bo", "g1", "s1", "b2", "g2", "s2")
MIB = 1024 * 1024

ANY = pl.BlockSpec(memory_space=pl.ANY)


def dot(a, b):
    return jnp.dot(a, b, preferred_element_type=F32)


def dot_nt(a, b):
    return lax.dot_general(a, b, (((1,), (1,)), ((), ())), preferred_element_type=F32)


def dot_tn(a, b):
    return lax.dot_general(a, b, (((0,), (0,)), ((), ())), preferred_element_type=F32)


def cost(flops, moved, transcendentals=0):
    return pl.CostEstimate(
        flops=int(flops),
        bytes_accessed=int(moved),
        transcendentals=int(transcendentals),
    )


def params(mib):
    return pltpu.CompilerParams(vmem_limit_bytes=mib * MIB)


def hbm(*arrays):
    return [pltpu.with_memory_space_constraint(x, pltpu.HBM) for x in arrays]


def once(shape, index):
    return pl.BlockSpec(shape, index, pipeline_mode=pl.Buffered(1))


def hop_z(x):
    size = lax.axis_size("fsdp")
    sends = x if isinstance(x, (list, tuple)) else [x] * 3
    return [
        lax.ppermute(send, "fsdp", [(i, i ^ (4 * d)) for i in range(size)])
        for d, send in enumerate(sends, 1)
    ]


def hop_plane(x, stage):
    size = lax.axis_size("fsdp")
    pairs = []
    for core in range(2):
        bit = 1 << (core ^ stage)
        pairs += [(core * size + i, core * size + (i ^ bit)) for i in range(size)]
    return lax.ppermute(x, AXES, pairs)


def hop_core(x):
    return lax.ppermute(x, "seq", [(0, 1), (1, 0)])


def place():
    me = lax.axis_index("fsdp")
    return me >> 2, (me >> 1) & 1, me & 1


def plane_bits():
    _, yi, xi = place()
    side = lax.axis_index("seq")
    return jnp.where(side == 0, xi, yi), jnp.where(side == 0, yi, xi)


def row_of(z, first, second):
    side = lax.axis_index("seq")
    return z * 4 + jnp.where(side == 0, second * 2 + first, first * 2 + second)


def local(kernel, arrays, shapes, after, name):
    moved = sum(2 * a.size for a in arrays) + sum(2 * math.prod(x) for x in shapes)
    whole = pl.BlockSpec(memory_space=pltpu.VMEM)
    return pl.pallas_call(
        kernel,
        out_shape=tuple(jax.ShapeDtypeStruct(x, BF) for x in shapes),
        in_specs=[whole] * len(arrays) + [ANY] * len(after),
        out_specs=(whole,) * len(shapes),
        compiler_params=params(14),
        cost_estimate=cost(0, moved),
        name=name,
    )(*arrays, *after)


def pack_kernel(count, *refs):
    out_ref, at = refs[-1], 0
    for ref in refs[:count]:
        out_ref[:, at : at + ref.shape[1]] = ref[...]
        at += ref.shape[1]


def pack(arrays, after):
    shape = (arrays[0].shape[0], sum(a.shape[1] for a in arrays))
    kernel = functools.partial(pack_kernel, len(arrays))
    return local(kernel, arrays, (shape,), after, "pack")[0]


def merge_z_kernel(x_ref, g1_ref, g2_ref, g3_ref, *refs):
    out_ref = refs[-1]
    zi, _, _ = place()
    for d, ref in enumerate((x_ref, g1_ref, g2_ref, g3_ref)):
        out_ref[pl.ds(jnp.bitwise_xor(zi, d), 1)] = ref[...][None]


def merge_one_kernel(a_ref, g_ref, *refs):
    out_ref = refs[-1]
    bit, _ = plane_bits()
    out_ref[pl.ds(bit, 1)] = a_ref[...][None]
    out_ref[pl.ds(1 - bit, 1)] = g_ref[...][None]


def merge_two_kernel(a_ref, g_ref, *refs):
    out_ref = refs[-1]
    _, bit = plane_bits()
    for ref, second in ((a_ref, bit), (g_ref, 1 - bit)):
        for first in range(2):
            for z in range(4):
                out_ref[pl.ds(row_of(z, first, second), 1)] = ref[first, z][None]


def merge_z(x, g, after):
    return local(merge_z_kernel, [x] + g, ((4,) + x.shape,), after, "merge_z")[0]


def merge_one(a, g, after):
    return local(merge_one_kernel, [a, g], ((2,) + a.shape,), after, "merge_one")[0]


def merge_two(a, g, after):
    rows, columns = a.shape[2:]
    shapes = ((16, rows, columns),)
    out = local(merge_two_kernel, [a, g], shapes, after, "merge_two")[0]
    return out.reshape(16 * rows, columns)


def plus(x, y):
    return (x.astype(F32) + y.astype(F32)).astype(BF)


def split_one_kernel(keep_ref, got_ref, *refs):
    _, bit = plane_bits()
    for ref, second in zip(refs[-2:], (1 - bit, bit)):
        for first in range(2):
            for z in range(4):
                at = pl.ds(row_of(z, first, second), 1)
                ref[first, z] = plus(keep_ref[at], got_ref[at])[0]


def split_two_kernel(keep_ref, got_ref, *refs):
    bit, _ = plane_bits()
    for ref, first in zip(refs[-2:], (1 - bit, bit)):
        at = pl.ds(first, 1)
        ref[...] = plus(keep_ref[at], got_ref[at])[0]


def split_z_kernel(keep_ref, got_ref, *refs):
    zi, _, _ = place()
    for d, ref in enumerate(refs[-4:]):
        at = pl.ds(jnp.bitwise_xor(zi, d), 1)
        ref[...] = plus(keep_ref[at], got_ref[at])[0]


def split_one(keep, got, after):
    columns = keep.shape[1]
    keep, got = (x.reshape(16, -1, columns) for x in (keep, got))
    shape = (2, 4) + keep.shape[1:]
    return local(split_one_kernel, [keep, got], (shape,) * 2, after, "split_one")


def split_two(keep, got, after):
    shape = keep.shape[1:]
    return local(split_two_kernel, [keep, got], (shape,) * 2, after, "split_two")


def split_z(keep, got, after):
    shape = keep.shape[1:]
    return local(split_z_kernel, [keep, got], (shape,) * 4, after, "split_z")


def total_of(keep, got):
    total = keep.astype(F32)
    for term in got:
        total = total + term.astype(F32)
    return total


class Fetch:
    def __init__(self, pieces, target, sem, at, chunks, by_rows):
        self.pieces, self.target, self.sem, self.at = pieces, target, sem, at
        self.chunks, self.by_rows = chunks, by_rows
        self.side = lax.axis_index("seq")

    def copy(self, chunk, piece):
        source, slot = self.pieces[piece], self.at + chunk
        height, width = self.target.shape
        if self.by_rows:
            rows = height // self.chunks
            local = chunk % (self.chunks // 2) * rows
            return pltpu.make_async_copy(
                source.at[pl.ds(local, rows)],
                self.target.at[pl.ds(chunk * rows, rows)],
                self.sem.at[slot],
            )
        columns = width // self.chunks // LANES * LANES
        end = width if chunk == self.chunks - 1 else (chunk + 1) * columns
        cut = slice(chunk * columns, end)
        if len(self.pieces) == 1:
            return pltpu.make_async_copy(
                source.at[:, cut], self.target.at[:, cut], self.sem.at[slot]
            )
        core = self.side if piece == 0 else 1 - self.side
        start = pl.multiple_of(core * (height // 2), 16)
        return pltpu.make_async_copy(
            source.at[:, cut],
            self.target.at[pl.ds(start, height // 2), cut],
            self.sem.at[slot + piece * self.chunks],
        )

    def start(self, chunk):
        if not self.by_rows:
            for piece in range(len(self.pieces)):
                self.copy(chunk, piece).start()
            return
        core = chunk // (self.chunks // 2)

        @pl.when(self.side == core)
        def _():
            self.copy(chunk, 0).start()

        @pl.when(self.side != core)
        def _():
            self.copy(chunk, 1).start()

    def wait(self, chunk):
        for piece in range(1 if self.by_rows else len(self.pieces)):
            self.copy(chunk, piece).wait()


def in_steps(body, *copies):
    @pl.when(pl.program_id(0) == 0)
    def _():
        for fetch, chunk in copies:
            fetch.start(chunk)
        body(True)

    @pl.when(pl.program_id(0) != 0)
    def _():
        body(False)


def project_kernel(x_ref, bias_ref, *refs):
    pieces, (q_ref, k_ref, v_ref), (w, sem) = refs[:2], refs[-5:-2], refs[-2:]
    width = x_ref.shape[1]
    fetch = Fetch(pieces, w, sem, 0, 3, False)

    def body(first):
        x = x_ref[...]
        if first:
            fetch.wait(0)
        q = (dot(x, w[:, :width]) + bias_ref[0:1, :]).astype(BF)
        q_ref[...] = (q.astype(F32) * HD ** (-0.5)).astype(BF)
        if first:
            fetch.wait(1)
        k_ref[...] = dot(x, w[:, width : 2 * width]).astype(BF)
        if first:
            fetch.wait(2)
        v = dot(x, w[:, 2 * width : 3 * width]) + bias_ref[1:2, :]
        v_ref[...] = v.astype(BF)

    in_steps(body, *[(fetch, i) for i in range(3)])


def project(flat, bias, pieces, after):
    rows, width = flat.shape
    columns = pieces[0].shape[1]
    block = pl.BlockSpec((BLOCK, width), lambda i: (i, 0))
    out = jax.ShapeDtypeStruct(flat.shape, BF)
    return pl.pallas_call(
        project_kernel,
        grid=(rows // BLOCK,),
        out_shape=(out,) * 3,
        in_specs=[block, once(bias.shape, lambda i: (0, 0))] + [ANY] * (2 + len(after)),
        out_specs=(block,) * 3,
        scratch_shapes=[
            pltpu.VMEM((width, columns), BF),
            pltpu.SemaphoreType.DMA((6,)),
        ],
        compiler_params=params(16),
        cost_estimate=cost(6 * rows * width * width, 20 * rows * width),
        name="project",
    )(flat, bias, *pieces, *after)


def lane_masks(rows):
    lane = lax.broadcasted_iota(jnp.int32, (rows, LANES), 1)
    return [lane < HD, lane >= HD]


def key_bias(valid):
    at = lax.broadcasted_iota(jnp.int32, (SEG, 1), 0)
    keep = (at < MEM) | (at >= SEG - MEM) | (at - MEM < valid)
    return jnp.where(keep, 0.0, -1000000000.0)


def attend_kernel(segment, valid_ref, q_ref, k_ref, v_ref, *refs):
    o_ref, log_ref = refs[-2:]
    bias = key_bias(valid_ref[segment]).astype(BF)
    q, k, v = q_ref[...], k_ref[...], v_ref[...]
    lane = lax.broadcasted_iota(jnp.int32, (SEG, LANES), 1)
    heads = q.shape[1] // HD

    def score(h):
        at = slice(h // 2 * LANES, (h // 2 + 1) * LANES)
        mask = (lane < HD) == (h % 2 == 0)
        spare = lane == (1 - h % 2) * HD
        return dot_nt(
            jnp.where(mask, k[:, at], jnp.where(spare, bias, 0)),
            jnp.where(mask, q[:, at], jnp.where(spare, 1, 0).astype(BF)),
        )

    vt = v.T
    outs = []
    ahead = score(0)
    for h in range(heads):
        scores = ahead
        if h + 1 < heads:
            ahead = score(h + 1)
        top = jnp.max(scores, axis=0, keepdims=True)
        weights = jnp.exp(scores - top)
        total = jnp.sum(weights, axis=0, keepdims=True)
        mixed = dot(vt[h * HD : (h + 1) * HD], weights.astype(BF))
        outs.append(mixed * (1.0 / total))
        log_ref[h // 2, h % 2 : h % 2 + 1, :] = top + jnp.log(total)
    o_ref[...] = jnp.concatenate(outs, axis=0).T.astype(BF)


def attend(segment, valid, q, k, v, earlier, after):
    rows, width = q.shape
    count, pairs = rows // SEG, width // LANES
    block = pl.BlockSpec((SEG, 2 * LANES), lambda p, _: (segment, p))
    return pl.pallas_call(
        functools.partial(attend_kernel, segment),
        grid_spec=pltpu.PrefetchScalarGridSpec(
            num_scalar_prefetch=1,
            grid=(pairs // 2,),
            in_specs=[block] * 3 + [ANY] * (len(earlier) + len(after)),
            out_specs=[
                block,
                pl.BlockSpec((2, 8, SEG), lambda p, _: (segment * pairs // 2 + p, 0, 0)),
            ],
        ),
        out_shape=(
            jax.ShapeDtypeStruct(q.shape, BF),
            jax.ShapeDtypeStruct((count * pairs, 8, SEG), F32),
        ),
        input_output_aliases={4 + i: i for i in range(len(earlier))},
        compiler_params=params(16),
        cost_estimate=cost(16 * SEG * SEG * width, 8 * SEG * width),
        name="attend",
    )(valid, q, k, v, *earlier, *after)


def attend_back_kernel(segment, valid_ref, q_ref, k_ref, v_ref, g_ref, log_ref, *refs):
    out_ref, sum_ref = refs[-2:]
    bias = key_bias(valid_ref[segment]).astype(BF)
    q, k, v, g = q_ref[...], k_ref[...], v_ref[...], g_ref[...]
    lane = lax.broadcasted_iota(jnp.int32, (SEG, LANES), 1)
    left = lane < HD
    heads = q.shape[1] // HD

    def start(h):
        at = slice(h // 2 * LANES, (h // 2 + 1) * LANES)
        mask = left == (h % 2 == 0)
        spare = lane == (1 - h % 2) * HD
        scores = dot_nt(
            jnp.where(mask, k[:, at], jnp.where(spare, bias, 0)),
            jnp.where(mask, q[:, at], jnp.where(spare, 1, 0).astype(BF)),
        )
        return scores, dot_nt(v[:, at], jnp.where(mask, g[:, at], 0))

    gq, gk, gv = [], [], []
    ahead = start(0)
    for h in range(heads):
        scores, g_probs = ahead
        if h + 1 < heads:
            ahead = start(h + 1)
        at = slice(h // 2 * LANES, (h // 2 + 1) * LANES)
        probs = jnp.exp(scores - log_ref[h // 2, h % 2 : h % 2 + 1, :])
        delta = jnp.sum(probs * g_probs, axis=0, keepdims=True)
        g_scores = (probs * (g_probs - delta)).astype(BF)
        gv.append(dot(probs.astype(BF), g[:, at]))
        gk.append(dot(g_scores, q[:, at]))
        gq.append(dot_tn(g_scores, k[:, at]))

    def both(parts, scale=1.0):
        pairs = range(0, heads, 2)
        return jnp.concatenate(
            [jnp.where(left, parts[i], parts[i + 1]) * scale for i in pairs], axis=1
        ).astype(BF)

    gq, gk, gv = both(gq, HD ** (-0.5)), both(gk), both(gv)
    out_ref[0], out_ref[1], out_ref[2] = gq, gk, gv
    sum_ref[...] = jnp.concatenate(
        [row_sum(gq.astype(F32)), row_sum(gv.astype(F32)), jnp.zeros((6, gq.shape[1]), F32)]
    )[None]


def attend_back(segment, valid, q, k, v, g, logs, after):
    rows, width = q.shape
    pairs = width // LANES
    block = pl.BlockSpec((SEG, 2 * LANES), lambda p, _: (segment, p))
    return pl.pallas_call(
        functools.partial(attend_back_kernel, segment),
        grid_spec=pltpu.PrefetchScalarGridSpec(
            num_scalar_prefetch=1,
            grid=(pairs // 2,),
            in_specs=[block] * 4
            + [pl.BlockSpec((2, 8, SEG), lambda p, _: (segment * pairs // 2 + p, 0, 0))]
            + [ANY] * len(after),
            out_specs=[
                pl.BlockSpec((3, SEG, 2 * LANES), lambda p, _: (0, 0, p)),
                pl.BlockSpec((1, 8, 2 * LANES), lambda p, _: (0, 0, p)),
            ],
        ),
        out_shape=(
            pltpu.HBM((3, SEG, width), BF),
            jax.ShapeDtypeStruct((1, 8, width), F32),
        ),
        compiler_params=params(24),
        cost_estimate=cost(20 * SEG * SEG * width, 14 * SEG * width),
        name="attend_back",
    )(valid, *hbm(q, k, v, g, logs), *after)


def normalize(resid):
    centre = resid - jnp.mean(resid, axis=-1, keepdims=True)
    inverse = lax.rsqrt(jnp.mean(centre * centre, axis=-1, keepdims=True) + EPSILON)
    return centre * inverse, inverse


def norm_back(grad_out, normed, inverse, gain):
    scaled = grad_out * gain
    return inverse * (
        scaled
        - jnp.mean(scaled, axis=-1, keepdims=True)
        - normed * jnp.mean(scaled * normed, axis=-1, keepdims=True)
    )


def gelu_parts(inner):
    phi = 0.5 * (1.0 + lax.erf(inner * ROOT_HALF))
    slope = phi + inner * (jnp.exp(-0.5 * inner * inner) * INV_ROOT_TAU)
    return inner * phi, slope


def row_sum(x):
    return jnp.sum(x, axis=0, keepdims=True)


def accumulate(ref, rows, first):
    stack = jnp.concatenate(
        rows + [jnp.zeros((8 - len(rows), rows[0].shape[1]), F32)], axis=0
    )
    ref[...] = stack if first else ref[...] + stack


def expand_kernel(att_ref, x_ref, vec_ref, *refs):
    mid = refs[:1]
    first_ref, n1_ref, inv_ref, act_ref, slope_ref, w1, sem = refs[-7:]
    width = x_ref.shape[1]
    fetch = Fetch(mid, w1, sem, 0, 5, False)
    vec = lambda i: vec_ref[i : i + 1, :]

    def body(first):
        if first:
            fetch.wait(0)
        branch = dot(att_ref[...], w1[:, :width]) + vec(2)
        n1, inv1 = normalize(x_ref[...].astype(F32) + branch)
        first_low = (n1 * vec(3) + vec(4)).astype(BF)
        n1_ref[...] = n1
        inv_ref[...] = jnp.broadcast_to(inv1, inv_ref.shape)
        first_ref[...] = first_low
        for f in range(4):
            cut = slice(f * width, (f + 1) * width)
            if first:
                fetch.wait(f + 1)
            inner = dot(first_low, w1[:, (f + 1) * width : (f + 2) * width]) + vec(8 + f)
            active, slope = gelu_parts(inner)
            act_ref[:, cut] = active.astype(BF)
            slope_ref[:, cut] = slope.astype(BF)

    in_steps(body, *[(fetch, i) for i in range(5)])


def expand(att, flat, vec, mid, after):
    rows, width = flat.shape
    block = pl.BlockSpec((BLOCK, width), lambda i: (i, 0))
    wide = pl.BlockSpec((BLOCK, 4 * width), lambda i: (i, 0))
    narrow = pl.BlockSpec((BLOCK, LANES), lambda i: (i, 0))
    s = jax.ShapeDtypeStruct
    return pl.pallas_call(
        expand_kernel,
        grid=(rows // BLOCK,),
        in_specs=[block] * 2
        + [once(vec.shape, lambda i: (0, 0))]
        + [ANY] * (1 + len(after)),
        out_specs=(block, block, narrow, wide, wide),
        out_shape=(
            s((rows, width), BF),
            s((rows, width), F32),
            s((rows, LANES), F32),
            s((rows, 4 * width), BF),
            pltpu.HBM((rows, 4 * width), BF),
        ),
        scratch_shapes=[
            pltpu.VMEM((width, 5 * width), BF),
            pltpu.SemaphoreType.DMA((6,)),
        ],
        compiler_params=params(26),
        cost_estimate=cost(10 * rows * width * width, 40 * rows * width),
        name="expand",
    )(att, *hbm(flat), vec, *hbm(*mid), *after)


def contract_kernel(act_ref, n1_ref, cot_ref, vec_ref, *refs):
    low = refs[:2]
    out_ref, res_ref, gout_ref, sum_ref, w2, sem = refs[-6:]
    width = n1_ref.shape[1]
    fetch = Fetch(low, w2, sem, 0, 4, True)
    vec = lambda i: vec_ref[i : i + 1, :]

    def body(first_step):
        if first_step:
            outer = vec(5)
            for f in range(4):
                cut = slice(f * width, (f + 1) * width)
                fetch.wait(f)
                outer = outer + dot(act_ref[:, cut], w2[cut, :])
        else:
            outer = dot(act_ref[...], w2[...]) + vec(5)
        first = n1_ref[...] * vec(3) + vec(4)
        n2, inv2 = normalize(first + outer)
        out_ref[...] = (n2 * vec(6) + vec(7)).astype(BF)
        cot = cot_ref[...].astype(F32)
        res = norm_back(cot, n2, inv2, vec(6))
        res_ref[...] = res
        gout = res.astype(BF)
        gout_ref[...] = gout
        sums = [row_sum(cot * n2), row_sum(cot), row_sum(gout.astype(F32))]
        accumulate(sum_ref, sums, first_step)

    in_steps(body, *[(fetch, i) for i in range(4)])


def contract(active, n1, cot, vec, low, after):
    rows, width = n1.shape
    block = pl.BlockSpec((BLOCK, width), lambda i: (i, 0))
    wide = pl.BlockSpec((BLOCK, 4 * width), lambda i: (i, 0))
    s = jax.ShapeDtypeStruct
    return pl.pallas_call(
        contract_kernel,
        grid=(rows // BLOCK,),
        in_specs=[wide, block, block]
        + [once(vec.shape, lambda i: (0, 0))]
        + [ANY] * (2 + len(after)),
        out_specs=(block, block, block, pl.BlockSpec((8, width), lambda i: (0, 0))),
        out_shape=(
            s((rows, width), BF),
            pltpu.HBM((rows, width), F32),
            s((rows, width), BF),
            s((8, width), F32),
        ),
        scratch_shapes=[
            pltpu.VMEM((4 * width, width), BF),
            pltpu.SemaphoreType.DMA((9,)),
        ],
        compiler_params=params(22),
        cost_estimate=cost(8 * rows * width * width, 24 * rows * width),
        name="contract",
    )(active, n1, *hbm(cot), vec, *hbm(*low), *after)


def backward_kernel(gout_ref, res_ref, slope_ref, n1_ref, inv_ref, vec_ref, *refs):
    mid, low = refs[:1], refs[1:3]
    (
        ginner_ref, res1_ref, gbranch_ref, gatt_ref, wide_ref, sum_ref, w1, w2, sem,
    ) = refs[-9:]
    width = gout_ref.shape[1]
    up = Fetch(mid, w1, sem, 0, 5, False)
    down = Fetch(low, w2, sem, 5, 4, True)
    copies = []
    for f in range(4):
        copies += [(down, f), (up, f + 1)]

    def body(first):
        def slopes(f):
            if first:
                down.wait(f)
            return dot_nt(gout, w2[f * width : (f + 1) * width, :])

        gout = gout_ref[...]
        g_first = res_ref[...]
        sums = []
        for f in range(4):
            cut = slice(f * width, (f + 1) * width)
            g_active = slopes(f)
            g_inner = (g_active * slope_ref[:, cut].astype(F32)).astype(BF)
            ginner_ref[:, cut] = g_inner
            sums.append(row_sum(g_inner.astype(F32)))
            if first:
                up.wait(f + 1)
            g_first = g_first + dot_nt(g_inner, w1[:, (f + 1) * width : (f + 2) * width])
        accumulate(wide_ref, sums, first)
        n1 = n1_ref[...]
        res1 = norm_back(g_first, n1, inv_ref[:, 0:1], vec_ref[3:4, :])
        res1_ref[...] = res1
        g_branch = res1.astype(BF)
        gbranch_ref[...] = g_branch
        if first:
            up.wait(0)
        gatt_ref[...] = dot_nt(g_branch, w1[:, :width]).astype(BF)
        sums = [row_sum(g_first * n1), row_sum(g_first), row_sum(g_branch.astype(F32))]
        accumulate(sum_ref, sums, first)

    in_steps(body, *copies, (up, 0))


def backward(gout, res, slope, n1, inv, vec, mid, low, after):
    rows, width = gout.shape
    block = pl.BlockSpec((BLOCK, width), lambda i: (i, 0))
    wide = pl.BlockSpec((BLOCK, 4 * width), lambda i: (i, 0))
    narrow = pl.BlockSpec((BLOCK, LANES), lambda i: (i, 0))
    sums = pl.BlockSpec((8, width), lambda i: (0, 0))
    s = jax.ShapeDtypeStruct
    return pl.pallas_call(
        backward_kernel,
        grid=(rows // BLOCK,),
        in_specs=[block, block, wide, block, narrow]
        + [once(vec.shape, lambda i: (0, 0))]
        + [ANY] * (3 + len(after)),
        out_specs=(wide, block, block, block, sums, sums),
        out_shape=(
            pltpu.HBM((rows, 4 * width), BF),
            pltpu.HBM((rows, width), F32),
            s((rows, width), BF),
            s((rows, width), BF),
            s((8, width), F32),
            s((8, width), F32),
        ),
        scratch_shapes=[
            pltpu.VMEM((width, 5 * width), BF),
            pltpu.VMEM((4 * width, width), BF),
            pltpu.SemaphoreType.DMA((9,)),
        ],
        compiler_params=params(36),
        cost_estimate=cost(18 * rows * width * width, 50 * rows * width),
        name="backward",
    )(gout, *hbm(res, slope, n1), inv, vec, *hbm(*mid, *low), *after)


def outer_grad_kernel(side_ref, far_ref, near_ref, g_ref, send_ref, keep_ref):
    g = g_ref[...]
    send_ref[...] = dot_tn(far_ref[...], g).astype(BF)
    keep_ref[...] = dot_tn(near_ref[...], g).astype(BF)


def outer_grad(side, active, gout):
    rows, width = gout.shape
    columns = active.shape[1]
    steps = columns // 2 // width
    out = pl.BlockSpec((width, width), lambda i, s: (i, 0))
    shape = jax.ShapeDtypeStruct((columns // 2, width), BF)
    return pl.pallas_call(
        outer_grad_kernel,
        grid_spec=pltpu.PrefetchScalarGridSpec(
            num_scalar_prefetch=1,
            grid=(steps,),
            in_specs=[
                pl.BlockSpec((rows, width), lambda i, s: (0, (1 - s[0]) * steps + i)),
                pl.BlockSpec((rows, width), lambda i, s: (0, s[0] * steps + i)),
                once((rows, width), lambda i, s: (0, 0)),
            ],
            out_specs=[out, out],
        ),
        out_shape=(shape, shape),
        compiler_params=params(22),
        cost_estimate=cost(2 * rows * columns * width, 2 * rows * columns),
        name="outer_grad",
    )(side, active, active, gout)


def inner_grad_kernel(side_ref, af_ref, an_ref, bf_ref, bn_ref, gi_ref, gb_ref, *refs):
    send_ref, keep_ref = refs[-2:]

    @pl.when(pl.program_id(0) == 0)
    def _():
        g = gb_ref[...]
        send_ref[...] = dot_tn(bf_ref[...], g).astype(BF)
        keep_ref[...] = dot_tn(bn_ref[...], g).astype(BF)

    @pl.when(pl.program_id(0) != 0)
    def _():
        g = gi_ref[...]
        send_ref[...] = dot_tn(af_ref[...], g).astype(BF)
        keep_ref[...] = dot_tn(an_ref[...], g).astype(BF)


def inner_grad(side, first, att, g_inner, g_branch, after):
    rows, width = first.shape
    half = width // 2
    near = once((rows, half), lambda i, s: (0, s[0]))
    far = once((rows, half), lambda i, s: (0, 1 - s[0]))
    out = pl.BlockSpec((half, width), lambda i, s: (0, i))
    shape = jax.ShapeDtypeStruct((half, 5 * width), BF)
    return pl.pallas_call(
        inner_grad_kernel,
        grid_spec=pltpu.PrefetchScalarGridSpec(
            num_scalar_prefetch=1,
            grid=(5,),
            in_specs=[far, near, far, near]
            + [
                pl.BlockSpec((rows, width), lambda i, s: (0, jnp.maximum(i - 1, 0))),
                once((rows, width), lambda i, s: (0, 0)),
            ]
            + [ANY] * len(after),
            out_specs=[out, out],
        ),
        out_shape=(shape, shape),
        compiler_params=params(22),
        cost_estimate=cost(10 * rows * width * width, 20 * rows * width),
        name="inner_grad",
    )(side, *hbm(first, first, att, att, g_inner), g_branch, *after)


def input_grad_kernel(side_ref, far_ref, near_ref, g0_ref, g1_ref, vf_ref, vn_ref, *refs):
    send_ref, keep_ref = refs[-2:]
    width = g0_ref.shape[-1]
    for i in range(3):

        @pl.when(pl.program_id(0) == i)
        def _(i=i):
            g = jnp.concatenate([g0_ref[0], g1_ref[0]])
            cut = slice(i * width, (i + 1) * width)
            send_ref[:, cut] = dot_tn(far_ref[...], g).astype(BF)
            keep_ref[:, cut] = dot_tn(near_ref[...], g).astype(BF)

    @pl.when(pl.program_id(0) == 0)
    def _():
        send_ref[:, 3 * width :] = vf_ref[...]
        keep_ref[:, 3 * width :] = vn_ref[...]


def input_grad(side, flat, g0, g1, vec, after):
    rows, width = flat.shape
    half = width // 2
    out = once((half, 3 * width + LANES), lambda i, s: (0, 0))
    shape = jax.ShapeDtypeStruct((half, 3 * width + LANES), BF)
    return pl.pallas_call(
        input_grad_kernel,
        grid_spec=pltpu.PrefetchScalarGridSpec(
            num_scalar_prefetch=1,
            grid=(3,),
            in_specs=[
                once((rows, half), lambda i, s: (0, 1 - s[0])),
                once((rows, half), lambda i, s: (0, s[0])),
                pl.BlockSpec((1, SEG, width), lambda i, s: (i, 0, 0)),
                pl.BlockSpec((1, SEG, width), lambda i, s: (i, 0, 0)),
                once((half, LANES), lambda i, s: (1 - s[0], 0)),
                once((half, LANES), lambda i, s: (s[0], 0)),
            ]
            + [ANY] * len(after),
            out_specs=[out, out],
        ),
        out_shape=(shape, shape),
        compiler_params=params(18),
        cost_estimate=cost(6 * rows * width * width, 10 * rows * width),
        name="input_grad",
    )(side, *hbm(flat, flat, g0, g1), vec, vec, *after)


def rows_grad_kernel(g0_ref, g1_ref, res_ref, *refs):
    pieces, (low_ref, mem_ref), (w, sem) = refs[:2], refs[-4:-2], refs[-2:]
    width = res_ref.shape[1]
    fetch = Fetch(pieces, w, sem, 0, 3, False)

    def body(first):
        total = res_ref[...]
        g_ref = g0_ref if first else g1_ref
        for i in range(3):
            if first:
                fetch.wait(i)
            total = total + dot_nt(g_ref[i], w[:, i * width : (i + 1) * width])
        low_ref[...] = total.astype(BF)
        mem_ref[0, :MEM] = total[:MEM] + total[SEG - 16 :][16 - MEM :]

    in_steps(body, *[(fetch, i) for i in range(3)])


def rows_grad(g0, g1, res, pieces, after):
    rows, width = res.shape
    columns = pieces[0].shape[1]
    count = rows // SEG
    block = pl.BlockSpec((SEG, width), lambda i: (i, 0))
    return pl.pallas_call(
        rows_grad_kernel,
        grid=(count,),
        in_specs=[once((3, SEG, width), lambda i: (0, 0, 0))] * 2 + [block]
        + [ANY] * (2 + len(after)),
        out_specs=(block, pl.BlockSpec((1, MEM, width), lambda i: (i, 0, 0))),
        out_shape=(
            jax.ShapeDtypeStruct((rows, width), BF),
            jax.ShapeDtypeStruct((count, MEM, width), F32),
        ),
        scratch_shapes=[
            pltpu.VMEM((width, columns), BF),
            pltpu.SemaphoreType.DMA((6,)),
        ],
        compiler_params=params(22),
        cost_estimate=cost(6 * rows * width * width, 12 * rows * width),
        name="rows_grad",
    )(*hbm(g0, g1, res, *pieces), *after)


def columns_of(vectors, rows):
    block = jnp.concatenate([jnp.stack(vectors[:-1]), vectors[-1].reshape(-1, rows)])
    return jnp.pad(block, ((0, LANES - block.shape[0]), (0, 0))).T


def whole_pieces(w, side):
    near, far = side * (w.shape[0] // 2), (1 - side) * (w.shape[0] // 2)
    cut = [
        lax.dynamic_slice_in_dim(w, at, w.shape[0] // 2, axis=0) for at in (near, far)
    ]
    return tuple(cut)


def per_device(tokens, read_memory, valid_count, cotangent, *parameters):
    side = lax.axis_index("seq")
    ring = lax.axis_size("fsdp") == 16
    p = dict(zip(NAMES, parameters))
    half = tokens.shape[0] // 2
    near = side * half
    far = (1 - side) * half
    width = tokens.shape[2]
    shard = p["Wq"].shape[0]
    side_ref = jnp.full((1,), side, jnp.int32)

    def take(x, at):
        return lax.dynamic_slice_in_dim(x, at, half, axis=0)

    def merge(x):
        own, got = take(x, near), hop_core(take(x, far))
        return jnp.where(side == 0, own, got), jnp.where(side == 0, got, own)

    mem = take(read_memory, near)
    valid = take(valid_count, near)
    low_tok, high_tok = merge(tokens)
    flat = jnp.concatenate([mem, low_tok, high_tok, mem], axis=1).reshape(-1, width)
    cot = jnp.concatenate(merge(cotangent), axis=1).reshape(-1, width)

    mid = pack([p["Wo"], p["W1"]], ())
    mid_shard = mid
    mid = (lax.all_gather(mid, AXES, axis=0, tiled=True),)
    if ring:
        vectors = columns_of([p[n] for n in VECTORS] + [p["b1"]], shard)
        top = pack([p["Wq"], p["Wk"], p["Wv"], vectors], [mid_shard])
        t = merge_z(top, hop_z(top), ())
        got = hop_plane(t, 0)
        low = pack([p["W2"]], [t])
        t = merge_one(t, got, [low, flat])
        low_z = hop_z(low)
        own = merge_two(t, hop_plane(t, 1), [*low_z, cot])
        top = (own, hop_core(own))
        tail = [t[:, -LANES:] for t in top]
        block = jnp.concatenate(
            [jnp.where(side == 0, tail[0], tail[1]), jnp.where(side == 0, tail[1], tail[0])]
        )
        vec = block[:, :16].astype(F32).T
        vec8 = vec[:8]
        inner = vec[8:12].reshape(4, 32, shard).transpose(1, 0, 2).reshape(4, width)
        vec = jnp.concatenate([vec[:8], inner, vec[12:]])
    else:
        full = {
            n: lax.all_gather(v, AXES, axis=0, tiled=True)
            for n, v in p.items()
            if n not in ("Wo", "W1")
        }
        blank = jnp.zeros((width, LANES), BF)
        top = jnp.concatenate([full["Wq"], full["Wk"], full["Wv"], blank], axis=1)
        top, low = (whole_pieces(w, side) for w in (top, full["W2"]))
        vec8 = vec = jnp.stack([full[n] for n in VECTORS]).astype(F32)
        vec = jnp.concatenate([vec, full["b1"].astype(F32).reshape(4, width)])
        vec = jnp.pad(vec, ((0, 4), (0, 0)))

    if ring:
        t = merge_z(low, low_z, [own])
        got = hop_plane(t, 0)
        q, k, v = project(flat, vec8, top, [t])
        t = merge_one(t, got, [v])
        got = hop_plane(t, 1)
        first_half = attend(0, valid, q, k, v, (), [t])
        att, logs = attend(1, valid, q, k, v, first_half, [])
        own = merge_two(t, got, [logs])
        low = (own, hop_core(own))
    else:
        q, k, v = project(flat, vec8, top, ())
        first_half = attend(0, valid, q, k, v, (), ())
        att, logs = attend(1, valid, q, k, v, first_half, ())
        own = logs
    first, n1, inv1, active, slope = expand(att, flat, vec, mid, [own])
    out, res2, gout, sum2 = contract(active, n1, cot, vec, low, ())
    send, keep = outer_grad(side_ref, active, gout)
    if ring:
        got = hop_core(send)
    g_inner, res1, g_branch, g_att, sum_b1, sum1 = backward(
        gout, res2, slope, n1, inv1, vec, mid, low, [keep]
    )
    if ring:
        w1_send, w1_keep = inner_grad(side_ref, first, att, g_inner, g_branch, [])
        w1_got = hop_core(w1_send)
        send, keep = split_one(keep, got, [w1_send])
        got = hop_plane(send, 1)
        g0, sum0 = attend_back(0, valid, q, k, v, g_att, logs, [send])
        send, keep = split_two(keep, got, [sum0])
        got = hop_plane(send, 0)
        w1_send, w1_keep = split_one(w1_keep, w1_got, [send])
        w1_got = hop_plane(w1_send, 1)
        g1, sum1_qv = attend_back(1, valid, q, k, v, g_att, logs, [w1_send])
        w2_keep, *sends = split_z(keep, got, [sum1_qv])
        w2_z = hop_z(sends)
        w1_send, w1_keep = split_two(w1_keep, w1_got, [w2_keep])
        w1_got = hop_plane(w1_send, 0)
    else:
        w1_send, w1_keep = inner_grad(side_ref, first, att, g_inner, g_branch, [])
        g0, sum0 = attend_back(0, valid, q, k, v, g_att, logs, ())
        g1, sum1_qv = attend_back(1, valid, q, k, v, g_att, logs, ())
        w2_keep = keep
    sum_qv = sum0[0] + sum1_qv[0]
    grads = [sum_qv[0], sum_qv[1], sum1[2], sum1[0], sum1[1], sum2[2], sum2[0], sum2[1]]
    if ring:
        b1 = sum_b1[:4].reshape(32, 4, shard).transpose(1, 0, 2).reshape(4, width)
        block = jnp.concatenate([jnp.stack(grads), b1]).astype(BF)
        block = jnp.pad(block, ((0, LANES - 12), (0, 0))).T
    else:
        block = jnp.zeros((width, LANES), BF)
    top_send, top_keep = input_grad(side_ref, flat, g0, g1, block, [w2_keep, w1_send])

    shards = {}
    if ring:
        got = hop_core(top_send)
        w1_keep, *sends = split_z(w1_keep, w1_got, [top_keep])
        w1_z = hop_z(sends)
        grad_low, grad_mem = rows_grad(g0, g1, res1, top, [w1_keep])
        top_send, top_keep = split_one(top_keep, got, [grad_mem])
        got = hop_plane(top_send, 1)
        top_send, top_keep = split_two(top_keep, got, w2_z)
        got = hop_plane(top_send, 0)
        top_keep, *sends = split_z(top_keep, got, w1_z)
        shards["W2"] = total_of(w2_keep, w2_z)
        got = total_of(w1_keep, w1_z)
        shards["Wo"], shards["W1"] = got[:, :width], got[:, width:]
        got = total_of(top_keep, hop_z(sends))
        for i, n in enumerate(("Wq", "Wk", "Wv")):
            shards[n] = got[:, i * width : (i + 1) * width]
        got = got[:, 3 * width : 3 * width + 12].T
        for i, n in enumerate(VECTORS):
            shards[n] = got[i]
        shards["b1"] = got[8:12].reshape(-1)
    else:
        grad_low, grad_mem = rows_grad(g0, g1, res1, top, [top_keep])

        def whole(send, keep):
            return jnp.concatenate(
                [jnp.where(side == 0, keep, send), jnp.where(side == 0, send, keep)]
            ).astype(F32)

        full = {"W2": whole(send, keep)}
        got = whole(w1_send, w1_keep)
        full["Wo"], full["W1"] = got[:, :width], got[:, width:]
        got = whole(top_send, top_keep)
        for i, n in enumerate(("Wq", "Wk", "Wv")):
            full[n] = got[:, i * width : (i + 1) * width]
        full.update(zip(VECTORS, grads))
        full["b1"] = sum_b1[:4].reshape(-1)
        for n, g in full.items():
            shards[n] = lax.psum_scatter(g, AXES, scatter_dimension=0, tiled=True)

    def back(low, high):
        own = jnp.where(side == 0, low, high)
        got = hop_core(jnp.where(side == 0, high, low))
        return jnp.concatenate(
            [jnp.where(side == 0, own, got), jnp.where(side == 0, got, own)]
        )

    middle = SEG // 2
    out = out.reshape(half, SEG, width)
    layer_out = back(out[:, :middle], out[:, middle:])
    grad_low = grad_low.reshape(half, SEG, width)
    tokens_grad = back(grad_low[:, MEM:middle], grad_low[:, middle : SEG - MEM])
    got = hop_core(grad_mem)
    memory_grad = jnp.concatenate(
        [jnp.where(side == 0, grad_mem, got), jnp.where(side == 0, got, grad_mem)]
    )
    return (layer_out, tokens_grad, memory_grad) + tuple(shards[n] for n in NAMES)


def solution(mesh):
    row = P("fsdp", "seq", None)
    whole = P("fsdp", None, None)
    mat, vec = P(AXES, None), P(AXES)
    specs = tuple(mat if n[0] == "W" else vec for n in NAMES)
    return jax.shard_map(
        per_device,
        mesh=mesh,
        in_specs=(row, whole, P("fsdp"), row) + specs,
        out_specs=(row, row, whole) + specs,
        check_vma=False,
    )
```
